256 devices in a mesh: row: 8 (over z_hi, core), col: 32 (over x, z_lo, y).
Axes of the slice: x: 4, y: 4, z: 8 (z_hi: 4, z_lo: 2; z = z_hi * 2 + z_lo), core: 2. Of those that a mesh axis runs over, the one named last changes fastest.
Arguments:
- data: bfloat16 [2, 110592, 4096], P(None, 'row', 'col'), may hold values from -0.59765625 to 0.59765625
- panel_cols: int32 [128], replicated, may hold values from 0 to 4095, as said below
- aperture: int32 [128, 24], replicated, may hold values from 0 to 863, as said below
- operator: float32 [2, 128], replicated, may hold values from -1.5 to 1.5
Outputs:
- predicted: bfloat16 [2, 4096, 128], P(None, ('row', 'col'))
- primaries: bfloat16 [2, 4096, 128], P(None, ('row', 'col'))
The draws below stay inside these ranges and needn't reach their ends.
Inputs may be any that keep to these rules, and one draw needn't show every extreme that they name: `panel_cols`: 128 distinct columns. `aperture`: each row holds 24 distinct tiles, all within 32 tiles of the tile that holds the source's trace tr(panel_cols[s]), counted around 864 tiles; that tile is one of them.
All inputs are finite; a program needn't handle non-finite values.
Results may differ from the reference program's by a relative error of at most 0.0065.
Values may be sent and summed in bfloat16 or wider, within the bound.
A program may use at most 128 MiB of HBM per device.

```python
import jax
import jax.numpy as jnp

NTR = 110592
TILE = 128
NA = 24
SPAN = 64
S = 128
RC_DEV = 128
ITERS = 2
K_DEV = 13824
WQ = 16
COLS = 4096
NTILES = 864
N_ROW = 8
N_COL = 32


def panel_pick(key):
    inner_cols = jax.random.permutation(key, COLS - 2)[:S - 2].astype(jnp.int32) + 1
    chosen = jnp.concatenate([jnp.array([0, COLS - 1], jnp.int32), inner_cols])
    order = jax.random.permutation(jax.random.fold_in(key, 11), S)
    return jnp.take(chosen, order).astype(jnp.int32)


def draw_panel_cols(key, part):
    chosen = panel_pick(key)
    return chosen


def offsets_one(subkey):
    shuffled = jax.random.permutation(subkey, SPAN - 2).astype(jnp.int32)[:NA - 2]
    moved = shuffled - SPAN // 2
    return moved + 2 * (moved >= -1).astype(jnp.int32)


def draw_aperture(key, part):
    chosen = panel_pick(key)
    key = jax.random.fold_in(key, 7)
    block = chosen // RC_DEV
    inner = chosen % RC_DEV
    traces = inner // WQ * K_DEV + block * WQ + inner % WQ
    center = traces // TILE
    subkeys = jax.random.split(key, S)
    rest = jax.vmap(offsets_one)(subkeys)
    fixed_part = jnp.stack([jnp.zeros((S,), jnp.int32), -jnp.ones((S,), jnp.int32)], axis=1)
    offsets = jnp.concatenate([fixed_part, rest], axis=1)
    return ((center[:, None] + offsets) % NTILES).astype(jnp.int32)


def levels(rng, shape, pieces, smallest, high):
    def one(dim, blocks):
        steps = jax.random.uniform(jax.random.fold_in(jax.random.fold_in(rng, 6), dim), (blocks,), jnp.float32, smallest / len(pieces), high / len(pieces))
        return jnp.repeat(jnp.exp(steps), shape[dim] // blocks).reshape((-1,) + (1,) * (len(shape) - dim - 1))

    factor_of = one(*pieces[0])
    for cut in pieces[1:]:
        factor_of = factor_of * one(*cut)
    return factor_of


def gaussian(own_key, extent, spread, bound, shards=(), kind=jnp.bfloat16):
    drawn = jax.random.normal(own_key, extent, jnp.float32) * spread
    if len(shards) > 0:
        drawn = levels(own_key, extent, shards, -0.22, 0.18) * drawn
    return jnp.clip(drawn, min=-bound, max=bound).astype(kind)


def setup_inputs(seed: int = 0) -> dict:
    splits = jax.random.split(jax.random.key(seed), 5)
    data = gaussian(splits[0], (2, NTR, COLS), ((2 * NA * TILE) ** -0.25), 0.59765625, ((1, 8), (2, 32)))
    panel_cols = draw_panel_cols(jax.random.fold_in(splits[4], 71), 0)
    aperture = draw_aperture(jax.random.fold_in(splits[4], 71), 0)
    operator = gaussian(splits[3], (2, S), 0.3, 1.5, (), jnp.float32)
    return dict(data=data, panel_cols=panel_cols, aperture=aperture, operator=operator)


def trace_of(column):
    block = column // RC_DEV
    inner = column % RC_DEV
    return (inner // WQ) * K_DEV + block * WQ + inner % WQ


def complex_scale(operator, multiples):
    real_part = operator[0][None, :] * multiples[0] - operator[1][None, :] * multiples[1]
    imag_part = operator[0][None, :] * multiples[1] + operator[1][None, :] * multiples[0]
    return jnp.stack([real_part, imag_part])


def predict(data, estimate):
    total_re = jnp.zeros((COLS, S), jnp.float32)
    total_im = jnp.zeros((COLS, S), jnp.float32)
    for block in range(N_ROW):
        rows = data[:, block * K_DEV:(block + 1) * K_DEV, :]
        panel = estimate[:, block * K_DEV:(block + 1) * K_DEV, :]
        total_re = total_re + jnp.dot(rows[0].T, panel[0], preferred_element_type=jnp.float32)
        total_re = total_re - jnp.dot(rows[1].T, panel[1], preferred_element_type=jnp.float32)
        total_im = total_im + jnp.dot(rows[0].T, panel[1], preferred_element_type=jnp.float32)
        total_im = total_im + jnp.dot(rows[1].T, panel[0], preferred_element_type=jnp.float32)
    return jnp.stack([total_re, total_im])


def reorder(values):
    shaped = values.reshape(2, N_COL, N_ROW, WQ, S)
    return jnp.transpose(shaped, (0, 2, 1, 3, 4)).reshape(2, COLS, S)


def reference(data, panel_cols, aperture, operator):
    columns = jnp.arange(COLS, dtype=jnp.int32)
    traces = trace_of(columns)
    tile_mask = jnp.max(jax.nn.one_hot(aperture, NTILES, dtype=jnp.float32), axis=1)
    tile_ids = jnp.arange(NTR, dtype=jnp.int32) // TILE
    mask = jnp.take(tile_mask, tile_ids, axis=1).astype(jnp.bfloat16)
    base = jnp.take(data, panel_cols, axis=2) * mask.T[None]
    window_mask = jnp.take(mask, traces, axis=1).T.astype(jnp.float32)
    window_base = jnp.take(base, traces, axis=1).astype(jnp.float32)
    estimate = base
    multiples = jnp.zeros((2, COLS, S), jnp.float32)
    window = window_base
    for step in range(ITERS):
        multiples = predict(data, estimate)
        window = window_base - window_mask[None] * complex_scale(operator, multiples)
        if step + 1 < ITERS:
            estimate = base.at[:, traces, :].set(window.astype(jnp.bfloat16))
    return reorder(multiples).astype(jnp.bfloat16), reorder(window).astype(jnp.bfloat16)
```

```python
import functools

import jax
import jax.numpy as jnp
from jax import lax
from jax.experimental import pallas as pl
from jax.experimental.pallas import tpu as pltpu
from jax.sharding import PartitionSpec as P

TILE = 128
ITERS = 2

MESH = pl.DeviceIdType.MESH
F32 = jnp.float32
BF16 = jnp.bfloat16
ROWS = 8
COLS = 32
BLOCK_TILES = 108
SIDE = 32
HEAD = 36
TAIL = 32
ACTIVE = HEAD + TAIL
QUOTA = 16
SLOTS = 32
GROUP = 8
GROUPS = COLS // GROUP
CHUNK = 32
LIST = GROUP * CHUNK
PAIRS = GROUPS * LIST
OWN = ACTIVE * QUOTA
WINDOW = COLS * QUOTA
HEAD_K = HEAD * TILE
TAIL_K = TAIL * TILE
TAIL_START = (BLOCK_TILES - TAIL) * TILE


def iota(shape, dim):
    return lax.broadcasted_iota(jnp.int32, shape, dim)


def dot(left, right):
    return jnp.dot(left.astype(BF16), right.astype(BF16), preferred_element_type=F32)


def prepare_kernel(cols_ref, ap_ref, op_ref, own_ref, pos_ref, key_ref, opa_ref, mask_ref, fit_ref):
    r = lax.axis_index("row")
    j = lax.axis_index("col")
    after = lax.rem(r + 1, ROWS)
    cols_row = cols_ref[...]
    sources = cols_row.shape[1]
    sub = iota((sources, sources), 0)
    lane = iota((sources, sources), 1)
    eye = sub == lane
    cols_col = jnp.sum(jnp.where(eye, cols_row.astype(F32), 0.0), axis=1, keepdims=True).astype(jnp.int32)
    row_row = (cols_row & 127) >> 4
    row_col = (cols_col & 127) >> 4
    dev_row = cols_row >> 7
    dev_col = cols_col >> 7
    same = row_row == row_col
    rank_row = jnp.sum(jnp.where(same & (sub < lane), 1.0, 0.0), axis=0, keepdims=True).astype(jnp.int32)
    rank_col = jnp.sum(jnp.where(same & (lane < sub), 1.0, 0.0), axis=1, keepdims=True).astype(jnp.int32)

    tile_id = jnp.where(lane < HEAD, lane + BLOCK_TILES * r, -1)
    in_tail = (lane >= 64) & (lane < 64 + TAIL)
    tile_id = jnp.where(in_tail, lane - 64 + BLOCK_TILES * r + BLOCK_TILES - TAIL, tile_id)
    hit = jnp.zeros((sources, sources), jnp.bool_)
    in_own = jnp.zeros((sources, 1), F32)
    low = row_col * BLOCK_TILES
    for n in range(ap_ref.shape[1]):
        tile = ap_ref[:, n:n + 1]
        hit = hit | (tile == tile_id)
        in_own = in_own + jnp.where((tile >= low) & (tile < low + BLOCK_TILES), 1.0, 0.0)
    hit = jnp.where(hit, 1.0, 0.0)

    wide = 2 * SLOTS
    slot = iota((wide, sources), 0)
    lane64 = iota((wide, sources), 1)
    is_head = slot < SLOTS
    want_row = jnp.where(is_head, r, after)
    want_rank = jnp.where(is_head, slot, slot - SLOTS)
    select = jnp.where((row_row == want_row) & (rank_row == want_rank), 1.0, 0.0)
    grid = dot(select, hit)
    grid = jnp.where(is_head == (lane64 < 64), grid, 0.0)
    before = dot(grid, jnp.where(sub < lane, 1.0, 0.0))
    count = jnp.sum(grid, axis=1, keepdims=True)
    group_of = jnp.where((dev_col >> 3) == lane, 1.0, 0.0)
    slot_group = dot(select, group_of)
    earlier = jnp.where(iota((wide, wide), 1) < iota((wide, wide), 0), 1.0, 0.0)
    running = dot(earlier, count * slot_group)
    offset = jnp.sum(slot_group * running, axis=1, keepdims=True)
    group_id = jnp.sum(slot_group * lane64.astype(F32), axis=1, keepdims=True)
    inside = before + offset
    valid = grid > 0.5
    pos_ref[...] = jnp.where(valid, inside + LIST * group_id, -1.0)

    slot_dev = jnp.sum(select * dev_row.astype(F32), axis=1, keepdims=True)
    slot_in = jnp.sum(select * (cols_row & 15).astype(F32), axis=1, keepdims=True)
    filled = jnp.sum(select, axis=1, keepdims=True) > 0.5
    mine = filled & (slot_dev == j.astype(F32))
    own_col = jnp.where(mine & (slot_in == lane64.astype(F32)), 1.0, 0.0)
    entry = iota((sources, OWN), 1)
    entry_tile = entry >> 4
    entry_lane = jnp.where(entry_tile < HEAD, entry_tile, entry_tile - HEAD + 64)
    spread = jnp.where(iota((sources, OWN), 0) == entry_lane, 1.0, 0.0)
    spread_col = jnp.where(iota((sources, OWN), 0) == (entry & 15), 1.0, 0.0)
    placed = jnp.where(valid, inside + 1.0, 0.0)
    own = jnp.sum(dot(placed, spread) * dot(own_col, spread_col), axis=0, keepdims=True) - 1.0
    own_ref[...] = jnp.broadcast_to(own, own_ref.shape)

    key_ref[...] = jnp.broadcast_to(row_row * TILE + rank_row, key_ref.shape)

    slot_lane = lane & (SLOTS - 1)
    place = jnp.where((row_col == r) & (rank_col == slot_lane) & (lane < 2 * SLOTS), 1.0, 0.0)
    op_re = jnp.sum(jnp.where(eye, op_ref[0:1, :], 0.0), axis=1, keepdims=True)
    op_im = jnp.sum(jnp.where(eye, op_ref[1:2, :], 0.0), axis=1, keepdims=True)
    same_part = jnp.sum(place * op_re, axis=0, keepdims=True)
    cross_part = jnp.sum(place * op_im, axis=0, keepdims=True)
    cross_part = jnp.where(lane[0:1] < SLOTS, -cross_part, cross_part)
    opa_ref[...] = jnp.concatenate([same_part, cross_part] + [jnp.zeros((6, sources), F32)], axis=0)
    window_tile = j >> 3
    mask_col = jnp.sum(jnp.where(lane == window_tile, hit, 0.0), axis=1, keepdims=True)
    mask_ref[...] = jnp.broadcast_to(jnp.sum(place * mask_col, axis=0, keepdims=True), mask_ref.shape)

    head_cell = row_col * GROUPS + (dev_col >> 3)
    tail_cell = ((row_col + ROWS - 1) & (ROWS - 1)) * GROUPS + (dev_col >> 3)
    total = float(ap_ref.shape[1])
    load = jnp.where(lane == head_cell, in_own, 0.0) + jnp.where(lane == tail_cell, total - in_own, 0.0)
    load = jnp.sum(load, axis=0, keepdims=True)
    over = jnp.where(load > LIST, 1.0, 0.0) + jnp.where(rank_row >= SLOTS, 1.0, 0.0)
    bad = jnp.sum(over)
    fit_ref[0, 0] = jnp.where(bad > 0.0, 0, 1)


def prepare(panel_cols, aperture, operator):
    sources = panel_cols.shape[0]
    vmem = pl.BlockSpec(memory_space=pltpu.VMEM)
    return pl.pallas_call(
        prepare_kernel,
        out_shape=(
            jax.ShapeDtypeStruct((8, OWN), F32),
            jax.ShapeDtypeStruct((2 * SLOTS, sources), F32),
            jax.ShapeDtypeStruct((8, sources), jnp.int32),
            jax.ShapeDtypeStruct((8, sources), F32),
            jax.ShapeDtypeStruct((8, sources), F32),
            jax.ShapeDtypeStruct((1, 1), jnp.int32),
        ),
        in_specs=[vmem] * 3,
        out_specs=[vmem] * 5 + [pl.BlockSpec(memory_space=pltpu.SMEM)],
    )(panel_cols.reshape(1, sources), aperture, operator)


def main_kernel(
    data_ref, own_ref, pos_ref, key_ref, opa_ref, mask_ref, pred_ref, prim_ref,
    head_ref, tail_ref, cols_ref, send_ref, recv_ref, chunk_ref, pairs_ref, pick_ref, est_ref,
    part_ref, carry_ref, turn_ref, fresh_ref, window_ref, out_ref, in_ref,
    load_sem, rs_send, rs_recv, ag_send, ag_recv, up_send, up_recv, fr_send, fr_recv, fin_send, fin_recv,
):
    r = lax.axis_index("row")
    j = lax.axis_index("col")
    x = j // GROUP
    y = j % GROUP
    after = lax.rem(r + 1, ROWS)
    before = lax.rem(r + ROWS - 1, ROWS)

    load_head = pltpu.make_async_copy(data_ref.at[:, pl.ds(0, HEAD_K), :], head_ref, load_sem.at[0])
    load_tail = pltpu.make_async_copy(data_ref.at[:, pl.ds(TAIL_START, TAIL_K), :], tail_ref, load_sem.at[1])
    load_head.start()
    load_tail.start()

    barrier = pltpu.get_barrier_semaphore()

    def greet_col(i, _):
        pl.semaphore_signal(barrier, inc=1, device_id=(r, (j + i) % COLS), device_id_type=MESH)
        return 0

    def greet_row(i, _):
        pl.semaphore_signal(barrier, inc=1, device_id=((r + i) % ROWS, j), device_id_type=MESH)
        return 0

    lax.fori_loop(1, COLS, greet_col, 0)
    lax.fori_loop(1, ROWS, greet_row, 0)

    line = iota((QUOTA, TILE), 0)
    where = iota((QUOTA, TILE), 1)

    def picker(first):
        hot = jnp.where(where == line + QUOTA * first, 1.0, 0.0).astype(BF16)
        none = jnp.zeros((QUOTA, TILE), BF16)
        return jnp.concatenate(
            [jnp.concatenate([hot, none], axis=1), jnp.concatenate([none, hot], axis=1)], axis=0
        )

    def extract(source, first, base):
        hot = picker(first)

        def body(i, _):
            rows = pl.ds(pl.multiple_of(i * 2 * TILE, 2 * TILE), 2 * TILE)
            block = jnp.concatenate([source[0, rows, :], source[1, rows, :]], axis=1)
            got = lax.dot_general(hot, block, (((1,), (1,)), ((), ())), preferred_element_type=F32).astype(BF16)
            for half in range(2):
                for part in range(2):
                    cols_ref[base + 2 * i + half, :, part * TILE:(part + 1) * TILE] = got[
                        part * QUOTA:(part + 1) * QUOTA, half * TILE:(half + 1) * TILE
                    ]
            return 0

        return body

    load_head.wait()
    lax.fori_loop(0, HEAD // 2, extract(head_ref, r, 0), 0)
    load_tail.wait()
    lax.fori_loop(0, TAIL // 2, extract(tail_ref, after, HEAD), 0)

    own = own_ref[0:1, :].astype(jnp.int32)
    gather = jnp.where(own == iota((LIST, OWN), 0), 1.0, 0.0).astype(BF16)
    listed = jnp.dot(gather, cols_ref[...].reshape(OWN, 2 * TILE), preferred_element_type=F32).astype(BF16)
    send_ref[...] = listed.reshape(GROUP, CHUNK, 2 * TILE)

    pl.semaphore_wait(barrier, COLS + ROWS - 2)

    def rs_copy(i):
        to = (y + i) % GROUP
        return pltpu.make_async_remote_copy(
            src_ref=send_ref.at[to], dst_ref=recv_ref.at[y], send_sem=rs_send.at[to], recv_sem=rs_recv.at[y],
            device_id=(r, x * GROUP + to), device_id_type=MESH,
        )

    def rs_start(i, _):
        rs_copy(i).start()
        return 0

    lax.fori_loop(1, GROUP, rs_start, 0)

    pos = pos_ref[...]

    def place_rows(first_lane, first_row, base):
        def body(t, _):
            turned = pltpu.roll(pos, lax.rem(2 * TILE - first_lane - t, TILE), 1)
            column = turned[first_row:first_row + SLOTS, 0:1].astype(jnp.int32)
            hot = jnp.where(column == iota((SLOTS, PAIRS), 1), 1.0, 0.0).astype(BF16)
            pick_ref[base + t] = hot
            return 0

        return body

    lax.fori_loop(0, HEAD, place_rows(0, 0, 0), 0)
    lax.fori_loop(0, TAIL, place_rows(64, SLOTS, HEAD), 0)

    def rs_wait(i, _):
        source = (y + i) % GROUP
        pltpu.make_async_remote_copy(
            src_ref=send_ref.at[source], dst_ref=recv_ref.at[source], send_sem=rs_send.at[source],
            recv_sem=rs_recv.at[source], device_id=(r, x * GROUP + source), device_id_type=MESH,
        ).wait()
        return 0

    lax.fori_loop(1, GROUP, rs_wait, 0)

    def rs_add(i, total):
        return total + recv_ref[(y + i) % GROUP].astype(F32)

    chunk_ref[...] = lax.fori_loop(1, GROUP, rs_add, send_ref[y].astype(F32)).astype(BF16)

    def spread(source_ref, target_ref, send_sem, recv_sem):
        def start(i, _):
            to = (j + i) % COLS
            pltpu.make_async_remote_copy(
                src_ref=source_ref, dst_ref=target_ref.at[j], send_sem=send_sem.at[to], recv_sem=recv_sem.at[j],
                device_id=(r, to), device_id_type=MESH,
            ).start()
            return 0

        def wait(i, _):
            other = (j + i) % COLS
            pltpu.make_async_remote_copy(
                src_ref=source_ref, dst_ref=target_ref.at[other], send_sem=send_sem.at[other],
                recv_sem=recv_sem.at[other], device_id=(r, other), device_id_type=MESH,
            ).wait()
            return 0

        return start, wait

    ag_start, ag_wait = spread(chunk_ref, pairs_ref, ag_send, ag_recv)
    lax.fori_loop(1, COLS, ag_start, 0)
    pairs_ref[j] = chunk_ref[...]
    lax.fori_loop(1, COLS, ag_wait, 0)

    step = ACTIVE // 4

    def expand(b, _):
        rows = pick_ref[pl.ds(b * step, step)].reshape(step * SLOTS, PAIRS)
        full = jnp.dot(rows, pairs_ref[...].reshape(PAIRS, 2 * TILE), preferred_element_type=F32).astype(BF16)
        full = full.reshape(step, SLOTS, 2 * TILE)
        est_ref[pl.ds(b * step, step), 0:SLOTS, :] = full[:, :, 0:TILE]
        est_ref[pl.ds(b * step, step), SLOTS:2 * SLOTS, :] = full[:, :, TILE:2 * TILE]
        return 0

    lax.fori_loop(0, 4, expand, 0)

    def multiply(source, base, first, last):
        def body(i, total):
            rows = pl.ds(pl.multiple_of(i * 2 * TILE, 2 * TILE), 2 * TILE)
            block = jnp.concatenate([source[0, rows, :], source[1, rows, :]], axis=1)
            left = jnp.concatenate([est_ref[base + 2 * i], est_ref[base + 2 * i + 1]], axis=1)
            return total + jnp.dot(left, block, preferred_element_type=F32)

        return lax.fori_loop(first, last, body, jnp.zeros((2 * SLOTS, 2 * TILE), F32))

    def fold(total):
        real = total[0:SLOTS, 0:TILE] - total[SLOTS:, TILE:]
        imag = total[0:SLOTS, TILE:] + total[SLOTS:, 0:TILE]
        return jnp.concatenate([real, imag], axis=0)

    part_ref[...] = fold(multiply(tail_ref, HEAD, 0, TAIL // 2))
    up = pltpu.make_async_remote_copy(
        src_ref=part_ref, dst_ref=carry_ref, send_sem=up_send, recv_sem=up_recv,
        device_id=(after, j), device_id_type=MESH,
    )
    up.start()
    window_tiles = WINDOW // TILE
    first_window = fold(multiply(head_ref, 0, 0, window_tiles // 2))
    rest = fold(multiply(head_ref, 0, window_tiles // 2, HEAD // 2))

    blank = jnp.zeros((TILE - 2 * SLOTS, TILE), F32)

    def turn(values):
        return jnp.concatenate([values, blank], axis=0).T

    lanes = iota((QUOTA, TILE), 1)

    def updated(base, multiples):
        swapped = jnp.where(
            lanes < SLOTS, pltpu.roll(multiples, TILE - SLOTS, 1), pltpu.roll(multiples, SLOTS, 1)
        )
        return base - mask_ref[0:1, :] * (opa_ref[0:1, :] * multiples + opa_ref[1:2, :] * swapped)

    turn_ref[...] = turn(est_ref[x].astype(F32)).reshape(ROWS, QUOTA, TILE)
    base16 = turn_ref[y]
    up.wait()
    rest = rest + carry_ref[...]
    turn_ref[...] = turn(rest + first_window).reshape(ROWS, QUOTA, TILE)
    fresh_ref[...] = updated(base16, turn_ref[r]).astype(BF16)

    fr_start, fr_wait = spread(fresh_ref, window_ref, fr_send, fr_recv)
    lax.fori_loop(1, COLS, fr_start, 0)
    window_ref[j] = fresh_ref[...]
    target = key_ref[0:1, :]
    target = jnp.concatenate([target, target + SLOTS], axis=1)
    scatter = jnp.where(target == iota((ROWS * TILE, 2 * TILE), 0), 1.0, 0.0).astype(BF16)
    source_row = key_ref[0:1, :] - r * TILE
    own_real = jnp.where(source_row == iota((TILE, TILE), 0), 1.0, 0.0)
    own_imag = jnp.where(source_row + SLOTS == iota((TILE, TILE), 0), 1.0, 0.0)
    in_row = (source_row >= 0) & (source_row < SLOTS)
    own_scatter = jnp.concatenate(
        [jnp.where(in_row, own_real, 0.0), jnp.where(in_row, own_imag, 0.0)], axis=1
    ).astype(BF16)
    lax.fori_loop(1, COLS, fr_wait, 0)

    def again(i, total):
        rows = pl.ds(pl.multiple_of(i * 2 * TILE, 2 * TILE), 2 * TILE)
        block = jnp.concatenate([head_ref[0, rows, :], head_ref[1, rows, :]], axis=1)
        left = window_ref[pl.ds(i * GROUP * 2, GROUP * 2)].reshape(2 * TILE, TILE)
        return total + lax.dot_general(left, block, (((0,), (0,)), ((), ())), preferred_element_type=F32)

    second = lax.fori_loop(0, window_tiles // 2, again, jnp.zeros((TILE, 2 * TILE), F32))
    total = rest + fold(second[0:2 * SLOTS])
    turn_ref[...] = turn(total).reshape(ROWS, QUOTA, TILE)
    out_ref[...] = turn_ref[...].astype(BF16)

    def fin_start(i, _):
        to = (r + i) % ROWS
        pltpu.make_async_remote_copy(
            src_ref=out_ref.at[to], dst_ref=in_ref.at[r], send_sem=fin_send.at[to], recv_sem=fin_recv.at[r],
            device_id=(to, j), device_id_type=MESH,
        ).start()
        return 0

    lax.fori_loop(1, ROWS, fin_start, 0)
    in_ref[r] = out_ref[r]
    final = updated(base16, turn_ref[r]).astype(BF16)
    mine = jnp.dot(final, own_scatter, preferred_element_type=F32).astype(BF16)
    prim_ref[0] = mine[:, 0:TILE]
    prim_ref[1] = mine[:, TILE:]

    def fin_wait(i, _):
        other = (r + i) % ROWS
        pltpu.make_async_remote_copy(
            src_ref=out_ref.at[other], dst_ref=in_ref.at[other], send_sem=fin_send.at[other],
            recv_sem=fin_recv.at[other], device_id=(other, j), device_id_type=MESH,
        ).wait()
        return 0

    lax.fori_loop(1, ROWS, fin_wait, 0)
    landed = jnp.concatenate([in_ref[k] for k in range(ROWS)], axis=1)
    result = jnp.dot(landed, scatter, preferred_element_type=F32).astype(BF16)
    pred_ref[0] = result[:, 0:TILE]
    pred_ref[1] = result[:, TILE:]


def compact(data, own, pos, key, opa, mask, *unused):
    sources = key.shape[1]
    vmem = pl.BlockSpec(memory_space=pltpu.VMEM)
    dma = pltpu.SemaphoreType.DMA
    return pl.pallas_call(
        main_kernel,
        out_shape=(jax.ShapeDtypeStruct((2, QUOTA, sources), BF16),) * 2,
        in_specs=[pl.BlockSpec(memory_space=pl.ANY)] + [vmem] * 5,
        out_specs=[vmem] * 2,
        scratch_shapes=[
            pltpu.VMEM((2, HEAD_K, TILE), BF16),
            pltpu.VMEM((2, TAIL_K, TILE), BF16),
            pltpu.VMEM((ACTIVE, QUOTA, 2 * TILE), BF16),
            pltpu.VMEM((GROUP, CHUNK, 2 * TILE), BF16),
            pltpu.VMEM((GROUP, CHUNK, 2 * TILE), BF16),
            pltpu.VMEM((CHUNK, 2 * TILE), BF16),
            pltpu.VMEM((COLS, CHUNK, 2 * TILE), BF16),
            pltpu.VMEM((ACTIVE, SLOTS, PAIRS), BF16),
            pltpu.VMEM((ACTIVE, 2 * SLOTS, TILE), BF16),
            pltpu.VMEM((2 * SLOTS, TILE), F32),
            pltpu.VMEM((2 * SLOTS, TILE), F32),
            pltpu.VMEM((ROWS, QUOTA, TILE), F32),
            pltpu.VMEM((QUOTA, TILE), BF16),
            pltpu.VMEM((COLS, QUOTA, TILE), BF16),
            pltpu.VMEM((ROWS, QUOTA, TILE), BF16),
            pltpu.VMEM((ROWS, QUOTA, TILE), BF16),
            dma((2,)), dma((GROUP,)), dma((GROUP,)), dma((COLS,)), dma((COLS,)), dma, dma,
            dma((COLS,)), dma((COLS,)), dma((ROWS,)), dma((ROWS,)),
        ],
        compiler_params=pltpu.CompilerParams(
            collective_id=0, has_side_effects=True, vmem_limit_bytes=40 * 1024 * 1024
        ),
    )(data, own, pos, key, opa, mask)


def subtract(operator, multiples, base_rows, mask_rows):
    sources = base_rows.shape[1]
    mult_re = multiples[:, :sources].T
    mult_im = multiples[:, sources:].T
    scale_re = operator[0][:, None]
    scale_im = operator[1][:, None]
    sub_re = scale_re * mult_re - scale_im * mult_im
    sub_im = scale_re * mult_im + scale_im * mult_re
    weight = mask_rows.astype(jnp.float32)[None]
    return base_rows.astype(jnp.float32) - weight * jnp.stack([sub_re, sub_im])


def general(data, panel_cols, aperture, operator):
    rows_dev = data.shape[1]
    receivers = data.shape[2]
    sources = panel_cols.shape[0]
    count_row = lax.axis_size("row")
    count_col = lax.axis_size("col")
    row_index = lax.axis_index("row")
    column_index = lax.axis_index("col")
    quota = receivers // count_row
    window = count_col * quota
    tile_count = rows_dev // TILE
    local_tiles = row_index * tile_count + jnp.arange(tile_count, dtype=jnp.int32)
    tile_hit = aperture[:, :, None] == local_tiles[None, None, :]
    tile_mask = jnp.any(tile_hit, axis=1)
    mask = jnp.repeat(tile_mask, TILE, axis=1).astype(jnp.bfloat16)
    own_columns = column_index * receivers + jnp.arange(receivers, dtype=jnp.int32)
    picker = (panel_cols[:, None] == own_columns[None, :]).astype(jnp.bfloat16)
    chosen = jnp.einsum("sc,zkc->zsk", picker, data, preferred_element_type=jnp.float32).astype(
        jnp.bfloat16
    )
    summed = lax.psum(chosen, "col").astype(jnp.float32)
    base = summed.astype(jnp.bfloat16) * mask[None]
    own_start = column_index * quota
    own_base = lax.dynamic_slice_in_dim(base, own_start, quota, 2)
    own_mask = lax.dynamic_slice_in_dim(mask, own_start, quota, 1)
    estimate = base
    piece = jnp.zeros((quota, 2 * sources), jnp.float32)
    for step in range(ITERS):
        current = estimate
        direct = jnp.einsum("zkc,zsk->zcs", data, current, preferred_element_type=jnp.float32)
        crossed = jnp.einsum(
            "zkc,zsk->zcs", data, current[::-1], preferred_element_type=jnp.float32
        )
        real_part = direct[0] - direct[1]
        imag_part = crossed[0] + crossed[1]
        piece = lax.psum_scatter(
            jnp.concatenate([real_part, imag_part], axis=1), "row", scatter_dimension=0, tiled=True
        )
        if step + 1 < ITERS:
            gathered = lax.all_gather(piece, "col", axis=0, tiled=True)
            fresh = subtract(operator, gathered, base[:, :, :window], mask[:, :window]).astype(
                jnp.bfloat16
            )
            estimate = jnp.concatenate([fresh, base[:, :, window:]], axis=2)
    final = subtract(operator, piece, own_base, own_mask)
    primaries = jnp.transpose(final, (0, 2, 1)).astype(jnp.bfloat16)
    predicted = jnp.transpose(piece.reshape(quota, 2, sources), (1, 0, 2)).astype(jnp.bfloat16)
    return (predicted, primaries)


def general_plan(data, own, pos, key, opa, mask, panel_cols, aperture, operator):
    return general(data, panel_cols, aperture, operator)


def shards(data, panel_cols, aperture, operator):
    *tables, fit = prepare(panel_cols, aperture, operator)
    return lax.cond(fit[0, 0] > 0, compact, general_plan, data, *tables, panel_cols, aperture, operator)


def solution(mesh):
    return jax.shard_map(
        shards,
        mesh=mesh,
        in_specs=(P(None, "row", "col"), P(), P(), P()),
        out_specs=(P(None, ("row", "col"), None), P(None, ("row", "col"), None)),
        check_vma=False,
    )
```

```python
import functools

import jax
import jax.numpy as jnp
from jax import lax
from jax.experimental import pallas as pl
from jax.experimental.pallas import tpu as pltpu
from jax.sharding import PartitionSpec as P

TILE = 128
ITERS = 2

MESH = pl.DeviceIdType.MESH
F32 = jnp.float32
BF16 = jnp.bfloat16
ROWS = 8
COLS = 32
BLOCK_TILES = 108
SIDE = 32
HEAD = 36
TAIL = 32
ACTIVE = HEAD + TAIL
QUOTA = 16
SLOTS = 32
GROUP = 8
GROUPS = COLS // GROUP
CHUNK = 32
LIST = GROUP * CHUNK
PAIRS = GROUPS * LIST
OWN = ACTIVE * QUOTA
WINDOW = COLS * QUOTA
HEAD_K = HEAD * TILE
TAIL_K = TAIL * TILE
TAIL_START = (BLOCK_TILES - TAIL) * TILE


def iota(shape, dim):
    return lax.broadcasted_iota(jnp.int32, shape, dim)


def dot(left, right):
    return jnp.dot(left.astype(BF16), right.astype(BF16), preferred_element_type=F32)


def make_tables(cols_ref, ap_ref, op_ref, own_ref, pos_ref, key_ref, opa_ref, mask_ref, fit_ref):
    r = lax.axis_index("row")
    j = lax.axis_index("col")
    after = lax.rem(r + 1, ROWS)
    cols_row = cols_ref[...]
    sources = cols_row.shape[1]
    sub = iota((sources, sources), 0)
    lane = iota((sources, sources), 1)
    eye = sub == lane
    cols_col = jnp.sum(jnp.where(eye, cols_row.astype(F32), 0.0), axis=1, keepdims=True).astype(jnp.int32)
    row_row = (cols_row & 127) >> 4
    row_col = (cols_col & 127) >> 4
    dev_row = cols_row >> 7
    dev_col = cols_col >> 7
    same = row_row == row_col
    rank_row = jnp.sum(jnp.where(same & (sub < lane), 1.0, 0.0), axis=0, keepdims=True).astype(jnp.int32)
    rank_col = jnp.sum(jnp.where(same & (lane < sub), 1.0, 0.0), axis=1, keepdims=True).astype(jnp.int32)

    tile_id = jnp.where(sub < HEAD, sub + BLOCK_TILES * r, -1)
    in_tail = (sub >= 64) & (sub < 64 + TAIL)
    tile_id = jnp.where(in_tail, sub - 64 + BLOCK_TILES * r + BLOCK_TILES - TAIL, tile_id)
    hit = jnp.zeros((sources, sources), jnp.bool_)
    for n in range(ap_ref.shape[0]):
        hit = hit | (ap_ref[n:n + 1, :] == tile_id)
    hit = jnp.where(hit, 1.0, 0.0)
    low = row_row * BLOCK_TILES
    tiles = ap_ref[...]
    in_own = jnp.where((tiles >= low) & (tiles < low + BLOCK_TILES), 1.0, 0.0)
    in_own = jnp.sum(in_own, axis=0, keepdims=True)

    wide = 2 * SLOTS
    slot = iota((wide, sources), 0)
    lane64 = iota((wide, sources), 1)
    is_head = slot < SLOTS
    want_row = jnp.where(is_head, r, after)
    want_rank = jnp.where(is_head, slot, slot - SLOTS)
    select = jnp.where((row_row == want_row) & (rank_row == want_rank), 1.0, 0.0)
    grid = lax.dot_general(
        select.astype(BF16), hit.astype(BF16), (((1,), (1,)), ((), ())), preferred_element_type=F32
    )
    grid = jnp.where(is_head == (lane64 < 64), grid, 0.0)
    before = dot(grid, jnp.where(sub < lane, 1.0, 0.0))
    count = jnp.sum(grid, axis=1, keepdims=True)
    group_of = jnp.where((dev_col >> 3) == lane, 1.0, 0.0)
    slot_group = dot(select, group_of)
    earlier = jnp.where(iota((wide, wide), 1) < iota((wide, wide), 0), 1.0, 0.0)
    running = dot(earlier, count * slot_group)
    offset = jnp.sum(slot_group * running, axis=1, keepdims=True)
    group_id = jnp.sum(slot_group * lane64.astype(F32), axis=1, keepdims=True)
    inside = before + offset
    valid = grid > 0.5
    pos_ref[...] = jnp.where(valid, inside + LIST * group_id, -1.0)

    slot_dev = jnp.sum(select * dev_row.astype(F32), axis=1, keepdims=True)
    slot_in = jnp.sum(select * (cols_row & 15).astype(F32), axis=1, keepdims=True)
    filled = jnp.sum(select, axis=1, keepdims=True) > 0.5
    mine = filled & (slot_dev == j.astype(F32))
    own_col = jnp.where(mine & (slot_in == lane64.astype(F32)), 1.0, 0.0)
    entry = iota((sources, OWN), 1)
    entry_tile = entry >> 4
    entry_lane = jnp.where(entry_tile < HEAD, entry_tile, entry_tile - HEAD + 64)
    spread = jnp.where(iota((sources, OWN), 0) == entry_lane, 1.0, 0.0)
    spread_col = jnp.where(iota((sources, OWN), 0) == (entry & 15), 1.0, 0.0)
    placed = jnp.where(valid, inside + 1.0, 0.0)
    own = jnp.sum(dot(placed, spread) * dot(own_col, spread_col), axis=0, keepdims=True) - 1.0
    own_ref[...] = jnp.broadcast_to(own, own_ref.shape)

    key_ref[...] = jnp.broadcast_to(row_row * TILE + rank_row, key_ref.shape)

    slot_lane = lane & (SLOTS - 1)
    place = jnp.where((row_col == r) & (rank_col == slot_lane) & (lane < 2 * SLOTS), 1.0, 0.0)
    op_re = jnp.sum(jnp.where(eye, op_ref[0:1, :], 0.0), axis=1, keepdims=True)
    op_im = jnp.sum(jnp.where(eye, op_ref[1:2, :], 0.0), axis=1, keepdims=True)
    same_part = jnp.sum(place * op_re, axis=0, keepdims=True)
    cross_part = jnp.sum(place * op_im, axis=0, keepdims=True)
    cross_part = jnp.where(lane[0:1] < SLOTS, -cross_part, cross_part)
    opa_ref[...] = jnp.concatenate([same_part, cross_part] + [jnp.zeros((6, sources), F32)], axis=0)
    window_tile = j >> 3
    mask_row = jnp.sum(jnp.where(sub == window_tile, hit, 0.0), axis=0, keepdims=True)
    mask_col = jnp.sum(jnp.where(eye, mask_row, 0.0), axis=1, keepdims=True)
    mask_ref[...] = jnp.broadcast_to(jnp.sum(place * mask_col, axis=0, keepdims=True), mask_ref.shape)

    cell = iota((ROWS * GROUPS, sources), 0)
    head_cell = row_row * GROUPS + (dev_row >> 3)
    tail_cell = ((row_row + ROWS - 1) & (ROWS - 1)) * GROUPS + (dev_row >> 3)
    total = float(ap_ref.shape[0])
    load = jnp.where(cell == head_cell, in_own, 0.0) + jnp.where(cell == tail_cell, total - in_own, 0.0)
    load = jnp.sum(load, axis=1, keepdims=True)
    bad = jnp.sum(jnp.where(load > LIST, 1.0, 0.0)) + jnp.sum(jnp.where(rank_row >= SLOTS, 1.0, 0.0))
    fit_ref[0, 0] = jnp.where(bad > 0.0, 0, 1)


def main_kernel(
    data_ref, cols_in_ref, ap_ref, op_ref, result_ref, fit_ref,
    own_ref, pos_ref, key_ref, opa_ref, mask_ref,
    head_ref, tail_ref, cols_ref, send_ref, recv_ref, chunk_ref, pairs_ref, pick_ref, est_ref,
    flip_ref, part_ref, carry_ref, first_ref, early_ref, turn_ref, fresh_ref, window_ref, out_ref, in_ref,
    load_sem, rs_send, rs_recv, ag_send, ag_recv, ur_send, ur_recv, up_send, up_recv, fr_send, fr_recv, fin_send, fin_recv,
):
    r = lax.axis_index("row")
    j = lax.axis_index("col")
    x = j // GROUP
    y = j % GROUP
    after = lax.rem(r + 1, ROWS)
    before = lax.rem(r + ROWS - 1, ROWS)

    load_head = pltpu.make_async_copy(data_ref.at[:, pl.ds(0, HEAD_K), :], head_ref, load_sem.at[0])
    load_tail = pltpu.make_async_copy(data_ref.at[:, pl.ds(TAIL_START, TAIL_K), :], tail_ref, load_sem.at[1])
    load_head.start()
    load_tail.start()

    barrier = pltpu.get_barrier_semaphore()

    def greet_col(i, _):
        pl.semaphore_signal(barrier, inc=1, device_id=(r, (j + i) % COLS), device_id_type=MESH)
        return 0

    def greet_row(i, _):
        pl.semaphore_signal(barrier, inc=1, device_id=((r + i) % ROWS, j), device_id_type=MESH)
        return 0

    lax.fori_loop(1, COLS, greet_col, 0)
    lax.fori_loop(1, ROWS, greet_row, 0)

    make_tables(cols_in_ref, ap_ref, op_ref, own_ref, pos_ref, key_ref, opa_ref, mask_ref, fit_ref)

    line = iota((QUOTA, TILE), 0)
    where = iota((QUOTA, TILE), 1)

    def picker(first):
        hot = jnp.where(where == line + QUOTA * first, 1.0, 0.0).astype(BF16)
        none = jnp.zeros((QUOTA, TILE), BF16)
        return jnp.concatenate(
            [jnp.concatenate([hot, none], axis=1), jnp.concatenate([none, hot], axis=1)], axis=0
        )

    def extract(source, first, base, width):
        hot = picker(first)

        def body(i, _):
            rows = pl.ds(pl.multiple_of(i * width * TILE, width * TILE), width * TILE)
            block = jnp.concatenate([source[0, rows, :], source[1, rows, :]], axis=1)
            got = lax.dot_general(hot, block, (((1,), (1,)), ((), ())), preferred_element_type=F32).astype(BF16)
            for t in range(width):
                for part in range(2):
                    cols_ref[base + width * i + t, :, part * TILE:(part + 1) * TILE] = got[
                        part * QUOTA:(part + 1) * QUOTA, t * TILE:(t + 1) * TILE
                    ]
            return 0

        return body

    load_head.wait()
    lax.fori_loop(0, HEAD // 12, extract(head_ref, r, 0, 12), 0)
    load_tail.wait()
    lax.fori_loop(0, TAIL // 8, extract(tail_ref, after, HEAD, 8), 0)

    own = own_ref[0:1, :].astype(jnp.int32)
    gather = jnp.where(own == iota((LIST, OWN), 0), 1.0, 0.0).astype(BF16)
    listed = jnp.dot(gather, cols_ref[...].reshape(OWN, 2 * TILE), preferred_element_type=F32).astype(BF16)
    send_ref[...] = listed.reshape(GROUP, CHUNK, 2 * TILE)

    pl.semaphore_wait(barrier, COLS + ROWS - 2)

    def rs_copy(i):
        to = (y + i) % GROUP
        return pltpu.make_async_remote_copy(
            src_ref=send_ref.at[to], dst_ref=recv_ref.at[y], send_sem=rs_send.at[to], recv_sem=rs_recv.at[y],
            device_id=(r, x * GROUP + to), device_id_type=MESH,
        )

    def rs_start(i, _):
        rs_copy(i).start()
        return 0

    lax.fori_loop(1, GROUP, rs_start, 0)

    pos = pos_ref[...]

    def place_rows(first_lane, first_row, base):
        def body(t, _):
            turned = pltpu.roll(pos, lax.rem(2 * TILE - first_lane - t, TILE), 1)
            column = turned[first_row:first_row + SLOTS, 0:1].astype(jnp.int32)
            hot = jnp.where(column == iota((SLOTS, PAIRS), 1), 1.0, 0.0).astype(BF16)
            for g in range(GROUPS):
                pick_ref[g, base + t] = hot[:, g * LIST:(g + 1) * LIST]
            return 0

        return body

    lax.fori_loop(0, HEAD, place_rows(0, 0, 0), 0, unroll=4)

    def rs_wait(i, _):
        source = (y + i) % GROUP
        pltpu.make_async_remote_copy(
            src_ref=send_ref.at[source], dst_ref=recv_ref.at[source], send_sem=rs_send.at[source],
            recv_sem=rs_recv.at[source], device_id=(r, x * GROUP + source), device_id_type=MESH,
        ).wait()
        return 0

    lax.fori_loop(1, GROUP, rs_wait, 0)

    def rs_add(i, total):
        return total + recv_ref[(y + i) % GROUP].astype(F32)

    chunk_ref[...] = lax.fori_loop(1, GROUP, rs_add, send_ref[y].astype(F32)).astype(BF16)

    def spread(source_ref, target_ref, send_sem, recv_sem):
        def copy(other, lands):
            return pltpu.make_async_remote_copy(
                src_ref=source_ref, dst_ref=target_ref.at[lands], send_sem=send_sem.at[other],
                recv_sem=recv_sem.at[lands], device_id=(r, other), device_id_type=MESH,
            )

        def member(step, i):
            return (x + step) % GROUPS * GROUP + (y + i) % GROUP

        def start(step):
            def body(i, _):
                copy(member(step, i), j).start()
                return 0

            lax.fori_loop(0 if step else 1, GROUP, body, 0)

        def wait(step):
            def body(i, _):
                other = member(step, i)
                copy(other, other).wait()
                return 0

            lax.fori_loop(0 if step else 1, GROUP, body, 0)

        return start, wait

    ag_start, ag_wait = spread(chunk_ref, pairs_ref, ag_send, ag_recv)
    for step in (2, 1, 3, 0):
        ag_start(step)
    pairs_ref[j] = chunk_ref[...]
    lax.fori_loop(0, TAIL, place_rows(64, SLOTS, HEAD), 0, unroll=4)

    window_data = jnp.concatenate([head_ref[0, 0:WINDOW, :], head_ref[1, 0:WINDOW, :]], axis=1)
    flip_ref[...] = window_data.T

    quarter = ACTIVE // 4

    def expand(step):
        group = (x + step) % GROUPS

        def body(b, _):
            rows = pick_ref[group, pl.ds(b * quarter, quarter)].reshape(quarter * SLOTS, LIST)
            held = pairs_ref[pl.ds(group * GROUP, GROUP)].reshape(LIST, 2 * TILE)
            full = jnp.dot(rows, held, preferred_element_type=F32).astype(BF16)
            for t in range(quarter):
                depth = pl.ds(pl.multiple_of((b * quarter + t) * TILE, TILE), TILE)
                for part in range(2):
                    lines = pl.ds(part * SLOTS, SLOTS)
                    value = full[t * SLOTS:(t + 1) * SLOTS, part * TILE:(part + 1) * TILE]
                    est_ref[lines, depth] = value if step == 0 else est_ref[lines, depth] + value
            return 0

        lax.fori_loop(0, 4, body, 0)

    for step in (0, 1, 3, 2):
        ag_wait(step)
        expand(step)

    def product(source, base, start, depth):
        rows = pl.ds(start, depth)
        block = jnp.concatenate([source[0, rows, :], source[1, rows, :]], axis=1)
        return jnp.dot(est_ref[:, pl.ds(base + start, depth)], block, preferred_element_type=F32)

    def multiply(source, base, start, depth, count):
        def body(i, total):
            return total + product(source, base, pl.multiple_of(start + i * depth, TILE), depth)

        return lax.fori_loop(0, count, body, jnp.zeros((2 * SLOTS, 2 * TILE), F32))

    def fold(total):
        real = total[0:SLOTS, 0:TILE] - total[SLOTS:, TILE:]
        imag = total[0:SLOTS, TILE:] + total[SLOTS:, 0:TILE]
        return jnp.concatenate([real, imag], axis=0)

    blank = jnp.zeros((TILE - 2 * SLOTS, TILE), F32)

    def turn(values):
        return jnp.concatenate([values, blank], axis=0).T

    part = fold(multiply(tail_ref, HEAD_K, 0, TAIL_K // 4, 4))
    part_ref[...] = part
    first_ref[...] = turn(part).reshape(ROWS, QUOTA, TILE)
    urgent = pltpu.make_async_remote_copy(
        src_ref=first_ref.at[after], dst_ref=early_ref, send_sem=ur_send, recv_sem=ur_recv,
        device_id=(after, j), device_id_type=MESH,
    )
    urgent.start()
    up = pltpu.make_async_remote_copy(
        src_ref=part_ref, dst_ref=carry_ref, send_sem=up_send, recv_sem=up_recv,
        device_id=(after, j), device_id_type=MESH,
    )
    up.start()
    first_window = fold(product(head_ref, 0, 0, WINDOW))
    rest = fold(multiply(head_ref, 0, WINDOW, (HEAD_K - WINDOW) // 4, 4))

    def swap(values):
        width = values.shape[0]
        left = pltpu.roll(values, TILE - SLOTS, 1)
        right = pltpu.roll(values, SLOTS, 1)
        return left, right, iota((width, TILE), 1) < SLOTS

    def updated(base, multiples):
        left, right, real = swap(multiples)
        swapped = jnp.where(real, left, right)
        return base - mask_ref[0:1, :] * (opa_ref[0:1, :] * multiples + opa_ref[1:2, :] * swapped)

    window_base = est_ref[:, pl.ds(pl.multiple_of(x * TILE, TILE), TILE)].astype(F32)
    turn_ref[...] = turn(window_base).reshape(ROWS, QUOTA, TILE)
    base16 = turn_ref[y]
    turn_ref[...] = turn(rest + first_window).reshape(ROWS, QUOTA, TILE)
    urgent.wait()
    fresh_ref[...] = updated(base16, turn_ref[r] + early_ref[...]).astype(BF16)

    fr_start, fr_wait = spread(fresh_ref, window_ref, fr_send, fr_recv)
    for step in (2, 1, 3, 0):
        fr_start(step)
    window_ref[j] = fresh_ref[...]
    target = key_ref[0:1, :]
    target = jnp.concatenate([target, target + SLOTS], axis=1)
    scatter = jnp.where(target == iota((ROWS * TILE, 2 * TILE), 0), 1.0, 0.0).astype(BF16)
    source_row = key_ref[0:1, :] - r * TILE
    own_real = jnp.where(source_row == iota((TILE, TILE), 0), 1.0, 0.0)
    own_imag = jnp.where(source_row + SLOTS == iota((TILE, TILE), 0), 1.0, 0.0)
    in_row = (source_row >= 0) & (source_row < SLOTS)
    own_scatter = jnp.concatenate(
        [jnp.where(in_row, own_real, 0.0), jnp.where(in_row, own_imag, 0.0)], axis=1
    ).astype(BF16)
    up.wait()
    rest = turn(rest + carry_ref[...])
    for step in (0, 1, 3, 2):
        fr_wait(step)

    second = jnp.dot(flip_ref[...], window_ref[...].reshape(WINDOW, TILE), preferred_element_type=F32)
    left, right, real = swap(second[TILE:])
    total = rest + second[0:TILE] + jnp.where(real, -left, right)
    total = jnp.where(iota((TILE, TILE), 1) < 2 * SLOTS, total, 0.0).reshape(ROWS, QUOTA, TILE)
    out_ref[...] = total.astype(BF16)
    turn_ref[...] = total

    def fin_start(i, _):
        to = (r + i) % ROWS
        pltpu.make_async_remote_copy(
            src_ref=out_ref.at[to], dst_ref=in_ref.at[r], send_sem=fin_send.at[to], recv_sem=fin_recv.at[r],
            device_id=(to, j), device_id_type=MESH,
        ).start()
        return 0

    lax.fori_loop(1, ROWS, fin_start, 0)
    in_ref[r] = out_ref[r]
    final = updated(base16, turn_ref[r]).astype(BF16)
    mine = jnp.dot(final, own_scatter, preferred_element_type=F32)
    result_ref[1, 0] = mine[:, 0:TILE]
    result_ref[1, 1] = mine[:, TILE:]

    def fin_wait(i, _):
        other = (r + i) % ROWS
        pltpu.make_async_remote_copy(
            src_ref=out_ref.at[other], dst_ref=in_ref.at[other], send_sem=fin_send.at[other],
            recv_sem=fin_recv.at[other], device_id=(other, j), device_id_type=MESH,
        ).wait()
        return 0

    lax.fori_loop(1, ROWS, fin_wait, 0)
    landed = jnp.concatenate([in_ref[k] for k in range(ROWS)], axis=1)
    predicted = jnp.dot(landed, scatter, preferred_element_type=F32)
    result_ref[0, 0] = predicted[:, 0:TILE]
    result_ref[0, 1] = predicted[:, TILE:]


def compact(data, panel_cols, aperture, operator):
    sources = panel_cols.shape[0]
    vmem = pl.BlockSpec(memory_space=pltpu.VMEM)
    dma = pltpu.SemaphoreType.DMA
    return pl.pallas_call(
        main_kernel,
        out_shape=(
            jax.ShapeDtypeStruct((2, 2, QUOTA, sources), F32),
            jax.ShapeDtypeStruct((1, 1), jnp.int32),
        ),
        in_specs=[pl.BlockSpec(memory_space=pl.ANY)] + [vmem] * 3,
        out_specs=[vmem, pl.BlockSpec(memory_space=pltpu.SMEM)],
        scratch_shapes=[
            pltpu.VMEM((8, OWN), F32),
            pltpu.VMEM((2 * SLOTS, sources), F32),
            pltpu.VMEM((8, sources), jnp.int32),
            pltpu.VMEM((8, sources), F32),
            pltpu.VMEM((8, sources), F32),
            pltpu.VMEM((2, HEAD_K, TILE), BF16),
            pltpu.VMEM((2, TAIL_K, TILE), BF16),
            pltpu.VMEM((ACTIVE, QUOTA, 2 * TILE), BF16),
            pltpu.VMEM((GROUP, CHUNK, 2 * TILE), BF16),
            pltpu.VMEM((GROUP, CHUNK, 2 * TILE), BF16),
            pltpu.VMEM((CHUNK, 2 * TILE), BF16),
            pltpu.VMEM((COLS, CHUNK, 2 * TILE), BF16),
            pltpu.VMEM((GROUPS, ACTIVE, SLOTS, LIST), BF16),
            pltpu.VMEM((2 * SLOTS, ACTIVE * TILE), BF16),
            pltpu.VMEM((2 * TILE, WINDOW), BF16),
            pltpu.VMEM((2 * SLOTS, TILE), F32),
            pltpu.VMEM((2 * SLOTS, TILE), F32),
            pltpu.VMEM((ROWS, QUOTA, TILE), F32),
            pltpu.VMEM((QUOTA, TILE), F32),
            pltpu.VMEM((ROWS, QUOTA, TILE), F32),
            pltpu.VMEM((QUOTA, TILE), BF16),
            pltpu.VMEM((COLS, QUOTA, TILE), BF16),
            pltpu.VMEM((ROWS, QUOTA, TILE), BF16),
            pltpu.VMEM((ROWS, QUOTA, TILE), BF16),
            dma((2,)), dma((GROUP,)), dma((GROUP,)), dma((COLS,)), dma((COLS,)), dma, dma, dma, dma,
            dma((COLS,)), dma((COLS,)), dma((ROWS,)), dma((ROWS,)),
        ],
        compiler_params=pltpu.CompilerParams(
            collective_id=0, has_side_effects=True, vmem_limit_bytes=40 * 1024 * 1024
        ),
    )(data, panel_cols.reshape(1, sources), aperture.T, operator)


def subtract(operator, multiples, base_rows, mask_rows):
    sources = base_rows.shape[1]
    mult_re = multiples[:, :sources].T
    mult_im = multiples[:, sources:].T
    scale_re = operator[0][:, None]
    scale_im = operator[1][:, None]
    sub_re = scale_re * mult_re - scale_im * mult_im
    sub_im = scale_re * mult_im + scale_im * mult_re
    weight = mask_rows.astype(jnp.float32)[None]
    return base_rows.astype(jnp.float32) - weight * jnp.stack([sub_re, sub_im])


def general(data, panel_cols, aperture, operator):
    rows_dev = data.shape[1]
    receivers = data.shape[2]
    sources = panel_cols.shape[0]
    count_row = lax.axis_size("row")
    count_col = lax.axis_size("col")
    row_index = lax.axis_index("row")
    column_index = lax.axis_index("col")
    quota = receivers // count_row
    window = count_col * quota
    tile_count = rows_dev // TILE
    local_tiles = row_index * tile_count + jnp.arange(tile_count, dtype=jnp.int32)
    tile_hit = aperture[:, :, None] == local_tiles[None, None, :]
    tile_mask = jnp.any(tile_hit, axis=1)
    mask = jnp.repeat(tile_mask, TILE, axis=1).astype(jnp.bfloat16)
    own_columns = column_index * receivers + jnp.arange(receivers, dtype=jnp.int32)
    picker = (panel_cols[:, None] == own_columns[None, :]).astype(jnp.bfloat16)
    chosen = jnp.einsum("sc,zkc->zsk", picker, data, preferred_element_type=jnp.float32).astype(
        jnp.bfloat16
    )
    summed = lax.psum(chosen, "col").astype(jnp.float32)
    base = summed.astype(jnp.bfloat16) * mask[None]
    own_start = column_index * quota
    own_base = lax.dynamic_slice_in_dim(base, own_start, quota, 2)
    own_mask = lax.dynamic_slice_in_dim(mask, own_start, quota, 1)
    estimate = base
    piece = jnp.zeros((quota, 2 * sources), jnp.float32)
    for step in range(ITERS):
        current = estimate
        direct = jnp.einsum("zkc,zsk->zcs", data, current, preferred_element_type=jnp.float32)
        crossed = jnp.einsum(
            "zkc,zsk->zcs", data, current[::-1], preferred_element_type=jnp.float32
        )
        real_part = direct[0] - direct[1]
        imag_part = crossed[0] + crossed[1]
        piece = lax.psum_scatter(
            jnp.concatenate([real_part, imag_part], axis=1), "row", scatter_dimension=0, tiled=True
        )
        if step + 1 < ITERS:
            gathered = lax.all_gather(piece, "col", axis=0, tiled=True)
            fresh = subtract(operator, gathered, base[:, :, :window], mask[:, :window]).astype(
                jnp.bfloat16
            )
            estimate = jnp.concatenate([fresh, base[:, :, window:]], axis=2)
    final = subtract(operator, piece, own_base, own_mask)
    primaries = jnp.transpose(final, (0, 2, 1)).astype(jnp.bfloat16)
    predicted = jnp.transpose(piece.reshape(quota, 2, sources), (1, 0, 2)).astype(jnp.bfloat16)
    return (predicted, primaries)


def shards(data, panel_cols, aperture, operator):
    result, fit = compact(data, panel_cols, aperture, operator)

    def keep(*_):
        return result

    def plan(*arguments):
        return jnp.stack(general(*arguments)).astype(F32)

    result = lax.cond(fit[0, 0] > 0, keep, plan, data, panel_cols, aperture, operator)
    return result[0].astype(BF16), result[1].astype(BF16)


def solution(mesh):
    return jax.shard_map(
        shards,
        mesh=mesh,
        in_specs=(P(None, "row", "col"), P(), P(), P()),
        out_specs=(P(None, ("row", "col"), None), P(None, ("row", "col"), None)),
        check_vma=False,
    )
```

```python
import functools

import jax
import jax.numpy as jnp
from jax import lax
from jax.experimental import pallas as pl
from jax.experimental.pallas import tpu as pltpu
from jax.sharding import PartitionSpec as P

TILE = 128
ITERS = 2

MESH = pl.DeviceIdType.MESH
F32 = jnp.float32
BF16 = jnp.bfloat16
ROWS = 8
COLS = 32
BLOCK_TILES = 108
SIDE = 32
HEAD = 36
TAIL = 32
ACTIVE = HEAD + TAIL
QUOTA = 16
SLOTS = 32
GROUP = 8
GROUPS = COLS // GROUP
CHUNK = 32
LIST = GROUP * CHUNK
PAIRS = GROUPS * LIST
OWN = ACTIVE * QUOTA
WINDOW = COLS * QUOTA
LOADS = 4
SIDE_X = 4
SIDE_Z = 2
HEAD_K = HEAD * TILE
TAIL_K = TAIL * TILE
TAIL_START = (BLOCK_TILES - TAIL) * TILE


def iota(shape, dim):
    return lax.broadcasted_iota(jnp.int32, shape, dim)


def dot(left, right):
    return jnp.dot(left.astype(BF16), right.astype(BF16), preferred_element_type=F32)


def make_tables(cols_ref, ap_ref, op_ref, own_ref, pos_ref, key_ref, opa_ref, mask_ref, fit_ref):
    r = lax.axis_index("row")
    j = lax.axis_index("col")
    after = lax.rem(r + 1, ROWS)
    cols_row = cols_ref[...]
    sources = cols_row.shape[1]
    sub = iota((sources, sources), 0)
    lane = iota((sources, sources), 1)
    eye = sub == lane
    cols_col = jnp.sum(jnp.where(eye, cols_row.astype(F32), 0.0), axis=1, keepdims=True).astype(jnp.int32)
    row_row = (cols_row & 127) >> 4
    row_col = (cols_col & 127) >> 4
    dev_row = cols_row >> 7
    dev_col = cols_col >> 7
    same = row_row == row_col
    rank_row = jnp.sum(jnp.where(same & (sub < lane), 1.0, 0.0), axis=0, keepdims=True).astype(jnp.int32)

    tile_id = jnp.where(sub < HEAD, sub + BLOCK_TILES * r, -1)
    in_tail = (sub >= 64) & (sub < 64 + TAIL)
    tile_id = jnp.where(in_tail, sub - 64 + BLOCK_TILES * r + BLOCK_TILES - TAIL, tile_id)
    hit = jnp.zeros((sources, sources), jnp.bool_)
    for n in range(ap_ref.shape[0]):
        hit = hit | (ap_ref[n:n + 1, :] == tile_id)
    hit = jnp.where(hit, 1.0, 0.0)
    low = row_row * BLOCK_TILES
    tiles = ap_ref[...]
    in_own = jnp.where((tiles >= low) & (tiles < low + BLOCK_TILES), 1.0, 0.0)
    in_own = jnp.sum(in_own, axis=0, keepdims=True)

    wide = 2 * SLOTS
    slot = iota((wide, sources), 0)
    lane64 = iota((wide, sources), 1)
    is_head = slot < SLOTS
    want_row = jnp.where(is_head, r, after)
    want_rank = jnp.where(is_head, slot, slot - SLOTS)
    select = jnp.where((row_row == want_row) & (rank_row == want_rank), 1.0, 0.0)
    grid = lax.dot_general(
        select.astype(BF16), hit.astype(BF16), (((1,), (1,)), ((), ())), preferred_element_type=F32
    )
    grid = jnp.where(is_head == (lane64 < 64), grid, 0.0)
    before = dot(grid, jnp.where(sub < lane, 1.0, 0.0))
    count = jnp.sum(grid, axis=1, keepdims=True)
    group_of = jnp.where((dev_col >> 3) == lane, 1.0, 0.0)
    slot_group = dot(select, group_of)
    earlier = jnp.where(iota((wide, wide), 1) < iota((wide, wide), 0), 1.0, 0.0)
    running = dot(earlier, count * slot_group)
    offset = jnp.sum(slot_group * running, axis=1, keepdims=True)
    inside = before + offset
    valid = grid > 0.5
    slot_dev = jnp.sum(select * dev_row.astype(F32), axis=1, keepdims=True)
    slot_in = jnp.sum(select * (cols_row & 15).astype(F32), axis=1, keepdims=True)
    filled = jnp.sum(select, axis=1, keepdims=True) > 0.5
    mine = filled & (slot_dev == j.astype(F32))
    own_col = jnp.where(mine & (slot_in == lane64.astype(F32)), 1.0, 0.0)
    entry = iota((sources, OWN), 1)
    entry_tile = entry >> 4
    entry_lane = jnp.where(entry_tile < HEAD, entry_tile, entry_tile - HEAD + 64)
    spread = jnp.where(iota((sources, OWN), 0) == entry_lane, 1.0, 0.0)
    spread_col = jnp.where(iota((sources, OWN), 0) == (entry & 15), 1.0, 0.0)
    placed = jnp.where(valid, inside + 1.0, 0.0)
    own = jnp.sum(dot(placed, spread) * dot(own_col, spread_col), axis=0, keepdims=True) - 1.0
    own_ref[...] = jnp.broadcast_to(own, own_ref.shape)

    def finish():
        rank_col = jnp.sum(jnp.where(same & (lane < sub), 1.0, 0.0), axis=1, keepdims=True).astype(jnp.int32)
        group_id = jnp.sum(slot_group * lane64.astype(F32), axis=1, keepdims=True)
        inner = inside.astype(jnp.int32)
        holder = inner >> 5
        order = (holder & 3) * GROUP + group_id.astype(jnp.int32) * 2 + (holder >> 2)
        pos_ref[...] = jnp.where(valid, (order * CHUNK + (inner & (CHUNK - 1))).astype(F32), -1.0)

        key_ref[...] = jnp.broadcast_to(row_row * TILE + rank_row, key_ref.shape)

        slot_lane = lane & (SLOTS - 1)
        place = jnp.where((row_col == r) & (rank_col == slot_lane) & (lane < 2 * SLOTS), 1.0, 0.0)
        op_re = jnp.sum(jnp.where(eye, op_ref[0:1, :], 0.0), axis=1, keepdims=True)
        op_im = jnp.sum(jnp.where(eye, op_ref[1:2, :], 0.0), axis=1, keepdims=True)
        same_part = jnp.sum(place * op_re, axis=0, keepdims=True)
        cross_part = jnp.sum(place * op_im, axis=0, keepdims=True)
        cross_part = jnp.where(lane[0:1] < SLOTS, -cross_part, cross_part)
        opa_ref[...] = jnp.concatenate([same_part, cross_part] + [jnp.zeros((6, sources), F32)], axis=0)
        window_tile = j >> 3
        mask_row = jnp.sum(jnp.where(sub == window_tile, hit, 0.0), axis=0, keepdims=True)
        mask_col = jnp.sum(jnp.where(eye, mask_row, 0.0), axis=1, keepdims=True)
        mask_ref[...] = jnp.broadcast_to(jnp.sum(place * mask_col, axis=0, keepdims=True), mask_ref.shape)

        cell = iota((ROWS * GROUPS, sources), 0)
        head_cell = row_row * GROUPS + (dev_row >> 3)
        tail_cell = ((row_row + ROWS - 1) & (ROWS - 1)) * GROUPS + (dev_row >> 3)
        total = float(ap_ref.shape[0])
        load = jnp.where(cell == head_cell, in_own, 0.0) + jnp.where(cell == tail_cell, total - in_own, 0.0)
        load = jnp.sum(load, axis=1, keepdims=True)
        bad = jnp.sum(jnp.where(load > LIST, 1.0, 0.0)) + jnp.sum(jnp.where(rank_row >= SLOTS, 1.0, 0.0))
        fit_ref[0, 0] = jnp.where(bad > 0.0, 0, 1)

    return finish


def main_kernel(
    data_ref, cols_in_ref, ap_ref, op_ref, result_ref, fit_ref,
    own_ref, pos_ref, key_ref, opa_ref, mask_ref,
    head_ref, tail_ref, cols_ref, send_ref, recv_ref, chunk_ref, pairs_ref, pick_ref, est_ref,
    flip_ref, part_ref, carry_ref, first_ref, early_ref, turn_ref, fresh_ref, window_ref, out_ref, in_ref,
    load_sem, rs_send, rs_recv, ag_send, ag_recv, ur_send, ur_recv, up_send, up_recv, fr_send, fr_recv, fin_send, fin_recv,
):
    r = lax.axis_index("row")
    j = lax.axis_index("col")
    x = j // GROUP
    y = j % GROUP
    z_at = y // SIDE_X
    y_at = y % SIDE_X
    after = lax.rem(r + 1, ROWS)
    before = lax.rem(r + ROWS - 1, ROWS)

    def load(i):
        part = i // LOADS
        piece = i % LOADS
        head = pl.ds(piece * (HEAD_K // LOADS), HEAD_K // LOADS)
        tail = pl.ds(piece * (TAIL_K // LOADS), TAIL_K // LOADS)
        far = pl.ds(TAIL_START + piece * (TAIL_K // LOADS), TAIL_K // LOADS)
        return (
            pltpu.make_async_copy(data_ref.at[part, head], head_ref.at[part, head], load_sem.at[0, i]),
            pltpu.make_async_copy(data_ref.at[part, far], tail_ref.at[part, tail], load_sem.at[1, i]),
        )

    for which in range(2):
        for i in range(2 * LOADS):
            load(i)[which].start()

    barrier = pltpu.get_barrier_semaphore()

    def greet_col(i, _):
        pl.semaphore_signal(barrier, inc=1, device_id=(r, (j + i) % COLS), device_id_type=MESH)
        return 0

    def greet_row(i, _):
        pl.semaphore_signal(barrier, inc=1, device_id=((r + i) % ROWS, j), device_id_type=MESH)
        return 0

    lax.fori_loop(1, COLS, greet_col, 0)
    lax.fori_loop(1, ROWS, greet_row, 0)

    finish_tables = make_tables(cols_in_ref, ap_ref, op_ref, own_ref, pos_ref, key_ref, opa_ref, mask_ref, fit_ref)

    line = iota((QUOTA, TILE), 0)
    where = iota((QUOTA, TILE), 1)

    def picker(first):
        hot = jnp.where(where == line + QUOTA * first, 1.0, 0.0).astype(BF16)
        none = jnp.zeros((QUOTA, TILE), BF16)
        return jnp.concatenate(
            [jnp.concatenate([hot, none], axis=1), jnp.concatenate([none, hot], axis=1)], axis=0
        )

    def extract(source, first, base, width):
        hot = picker(first)

        def body(i, _):
            rows = pl.ds(pl.multiple_of(i * width * TILE, width * TILE), width * TILE)
            block = jnp.concatenate([source[0, rows, :], source[1, rows, :]], axis=1)
            got = lax.dot_general(hot, block, (((1,), (1,)), ((), ())), preferred_element_type=F32).astype(BF16)
            for t in range(width):
                for part in range(2):
                    cols_ref[base + width * i + t, :, part * TILE:(part + 1) * TILE] = got[
                        part * QUOTA:(part + 1) * QUOTA, t * TILE:(t + 1) * TILE
                    ]
            return 0

        return body

    for i in range(2 * LOADS):
        load(i)[0].wait()
    lax.fori_loop(0, HEAD // 12, extract(head_ref, r, 0, 12), 0)
    for i in range(2 * LOADS):
        load(i)[1].wait()
    lax.fori_loop(0, TAIL // 8, extract(tail_ref, after, HEAD, 8), 0)

    own = own_ref[0:1, :].astype(jnp.int32)
    gather = jnp.where(own == iota((LIST, OWN), 0), 1.0, 0.0).astype(BF16)
    listed = jnp.dot(gather, cols_ref[...].reshape(OWN, 2 * TILE), preferred_element_type=F32).astype(BF16)
    send_ref[...] = listed.reshape(GROUP, CHUNK, 2 * TILE)

    pl.semaphore_wait(barrier, COLS + ROWS - 2)

    def rs_copy(i):
        to = (y + i) % GROUP
        return pltpu.make_async_remote_copy(
            src_ref=send_ref.at[to], dst_ref=recv_ref.at[y], send_sem=rs_send.at[to], recv_sem=rs_recv.at[y],
            device_id=(r, x * GROUP + to), device_id_type=MESH,
        )

    def rs_start(i, _):
        rs_copy(i).start()
        return 0

    for i in (6, 2, 5, 7, 4, 1, 3):
        rs_start(i, 0)

    finish_tables()

    pos = pos_ref[...]

    def place_rows(first_lane, first_row, base):
        def body(t, _):
            turned = pltpu.roll(pos, lax.rem(2 * TILE - first_lane - t, TILE), 1)
            column = turned[first_row:first_row + SLOTS, 0:1].astype(jnp.int32)
            hot = jnp.where(column == iota((SLOTS, PAIRS), 1), 1.0, 0.0).astype(BF16)
            for g in range(GROUPS):
                pick_ref[g, base + t] = hot[:, g * LIST:(g + 1) * LIST]
            return 0

        return body

    lax.fori_loop(0, HEAD, place_rows(0, 0, 0), 0, unroll=4)

    def rs_wait(i, _):
        source = (y + i) % GROUP
        pltpu.make_async_remote_copy(
            src_ref=send_ref.at[source], dst_ref=recv_ref.at[source], send_sem=rs_send.at[source],
            recv_sem=rs_recv.at[source], device_id=(r, x * GROUP + source), device_id_type=MESH,
        ).wait()
        return 0

    lax.fori_loop(1, GROUP, rs_wait, 0)

    def rs_add(i, total):
        return total + recv_ref[(y + i) % GROUP].astype(F32)

    chunk_ref[...] = lax.fori_loop(1, GROUP, rs_add, send_ref[y].astype(F32)).astype(BF16)

    def spread(source_ref, target_ref, send_sem, recv_sem, place):
        def copy(other, lands):
            return pltpu.make_async_remote_copy(
                src_ref=source_ref, dst_ref=target_ref.at[place(lands)], send_sem=send_sem.at[other],
                recv_sem=recv_sem.at[lands], device_id=(r, other), device_id_type=MESH,
            )

        def others(step):
            for a, b in ((2, 1), (2, 0), (1, 1), (3, 1), (1, 0), (3, 0), (0, 1), (0, 0)):
                if a or b or step:
                    yield (x + a) % SIDE_X * GROUP + (z_at + b) % SIDE_Z * SIDE_X + (y_at + step) % SIDE_X

        def start(step):
            for other in others(step):
                copy(other, j).start()

        def wait(step):
            for other in others(step):
                copy(other, other).wait_recv()

        def finish():
            for step in range(SIDE_X):
                for other in others(step):
                    copy(other, other).wait_send()

        return start, wait, finish

    def by_y(device):
        return device % SIDE_X * GROUP + device // GROUP * SIDE_Z + device // SIDE_X % SIDE_Z

    def as_is(device):
        return device

    ag_start, ag_wait, ag_finish = spread(chunk_ref, pairs_ref, ag_send, ag_recv, by_y)
    for step in (2, 1, 3, 0):
        ag_start(step)
    pairs_ref[by_y(j)] = chunk_ref[...]
    lax.fori_loop(0, TAIL, place_rows(64, SLOTS, HEAD), 0, unroll=4)

    window_data = jnp.concatenate([head_ref[0, 0:WINDOW, :], head_ref[1, 0:WINDOW, :]], axis=1)
    flip_ref[...] = window_data.T

    for step in (2, 1, 3, 0):
        ag_wait(step)

    def expand(first, tiles):
        def body(b, _):
            start = first + b * tiles
            rows = jnp.concatenate(
                [pick_ref[g, pl.ds(start, tiles)].reshape(tiles * SLOTS, LIST) for g in range(GROUPS)], axis=1
            )
            held = pairs_ref[...].reshape(PAIRS, 2 * TILE)
            full = jnp.dot(rows, held, preferred_element_type=F32).astype(BF16)
            for t in range(tiles):
                depth = pl.ds(pl.multiple_of((start + t) * TILE, TILE), TILE)
                est_ref[0:SLOTS, depth] = full[t * SLOTS:(t + 1) * SLOTS, 0:TILE]
                est_ref[SLOTS:2 * SLOTS, depth] = full[t * SLOTS:(t + 1) * SLOTS, TILE:2 * TILE]
            return 0

        lax.fori_loop(0, 2, body, 0)

    expand(HEAD, TAIL // 2)

    def product(source, base, start, depth):
        rows = pl.ds(start, depth)
        block = jnp.concatenate([source[0, rows, :], source[1, rows, :]], axis=1)
        return jnp.dot(est_ref[:, pl.ds(base + start, depth)], block, preferred_element_type=F32)

    def multiply(source, base, start, depth, count):
        def body(i, total):
            return total + product(source, base, pl.multiple_of(start + i * depth, TILE), depth)

        return lax.fori_loop(0, count, body, jnp.zeros((2 * SLOTS, 2 * TILE), F32))

    def fold(total):
        real = total[0:SLOTS, 0:TILE] - total[SLOTS:, TILE:]
        imag = total[0:SLOTS, TILE:] + total[SLOTS:, 0:TILE]
        return jnp.concatenate([real, imag], axis=0)

    blank = jnp.zeros((TILE - 2 * SLOTS, TILE), F32)

    def turn(values):
        return jnp.concatenate([values, blank], axis=0).T

    part = fold(multiply(tail_ref, HEAD_K, 0, TAIL_K // 4, 4))
    part_ref[...] = part
    first_ref[...] = turn(part).reshape(ROWS, QUOTA, TILE)
    urgent = pltpu.make_async_remote_copy(
        src_ref=first_ref.at[after], dst_ref=early_ref, send_sem=ur_send, recv_sem=ur_recv,
        device_id=(after, j), device_id_type=MESH,
    )
    urgent.start()
    up = pltpu.make_async_remote_copy(
        src_ref=part_ref, dst_ref=carry_ref, send_sem=up_send, recv_sem=up_recv,
        device_id=(after, j), device_id_type=MESH,
    )
    up.start()
    ag_finish()
    expand(0, HEAD // 2)
    first_window = fold(product(head_ref, 0, 0, WINDOW))
    rest = fold(multiply(head_ref, 0, WINDOW, (HEAD_K - WINDOW) // 4, 4))

    def swap(values):
        width = values.shape[0]
        left = pltpu.roll(values, TILE - SLOTS, 1)
        right = pltpu.roll(values, SLOTS, 1)
        return left, right, iota((width, TILE), 1) < SLOTS

    def updated(base, multiples):
        left, right, real = swap(multiples)
        swapped = jnp.where(real, left, right)
        return base - mask_ref[0:1, :] * (opa_ref[0:1, :] * multiples + opa_ref[1:2, :] * swapped)

    window_base = est_ref[:, pl.ds(pl.multiple_of(x * TILE, TILE), TILE)].astype(F32)
    turn_ref[...] = turn(window_base).reshape(ROWS, QUOTA, TILE)
    base16 = turn_ref[y]
    turn_ref[...] = turn(rest + first_window).reshape(ROWS, QUOTA, TILE)
    urgent.wait()
    fresh_ref[...] = updated(base16, turn_ref[r] + early_ref[...]).astype(BF16)

    fr_start, fr_wait, fr_finish = spread(fresh_ref, window_ref, fr_send, fr_recv, as_is)
    for step in (2, 1, 3, 0):
        fr_start(step)
    window_ref[j] = fresh_ref[...]
    target = key_ref[0:1, :]
    target = jnp.concatenate([target, target + SLOTS], axis=1)
    scatter = jnp.where(target == iota((ROWS * TILE, 2 * TILE), 0), 1.0, 0.0).astype(BF16)
    source_row = key_ref[0:1, :] - r * TILE
    own_real = jnp.where(source_row == iota((TILE, TILE), 0), 1.0, 0.0)
    own_imag = jnp.where(source_row + SLOTS == iota((TILE, TILE), 0), 1.0, 0.0)
    in_row = (source_row >= 0) & (source_row < SLOTS)
    own_scatter = jnp.concatenate(
        [jnp.where(in_row, own_real, 0.0), jnp.where(in_row, own_imag, 0.0)], axis=1
    ).astype(BF16)
    up.wait()
    rest = turn(rest + carry_ref[...])
    for step in (2, 1, 3, 0):
        fr_wait(step)

    second = jnp.dot(flip_ref[...], window_ref[...].reshape(WINDOW, TILE), preferred_element_type=F32)
    left, right, real = swap(second[TILE:])
    total = rest + second[0:TILE] + jnp.where(real, -left, right)
    total = jnp.where(iota((TILE, TILE), 1) < 2 * SLOTS, total, 0.0).reshape(ROWS, QUOTA, TILE)
    out_ref[...] = total.astype(BF16)
    turn_ref[...] = total

    def fin_start(i, _):
        to = (r + i) % ROWS
        pltpu.make_async_remote_copy(
            src_ref=out_ref.at[to], dst_ref=in_ref.at[r], send_sem=fin_send.at[to], recv_sem=fin_recv.at[r],
            device_id=(to, j), device_id_type=MESH,
        ).start()
        return 0

    for i in (4, 5, 3, 2, 6, 7, 1):
        fin_start(i, 0)
    in_ref[r] = out_ref[r]
    fr_finish()
    final = updated(base16, turn_ref[r]).astype(BF16)
    mine = jnp.dot(final, own_scatter, preferred_element_type=F32).astype(BF16)
    result_ref[1, 0] = mine[:, 0:TILE]
    result_ref[1, 1] = mine[:, TILE:]

    def fin_wait(i, _):
        other = (r + i) % ROWS
        pltpu.make_async_remote_copy(
            src_ref=out_ref.at[other], dst_ref=in_ref.at[other], send_sem=fin_send.at[other],
            recv_sem=fin_recv.at[other], device_id=(other, j), device_id_type=MESH,
        ).wait()
        return 0

    lax.fori_loop(1, ROWS, fin_wait, 0)
    landed = jnp.concatenate([in_ref[k] for k in range(ROWS)], axis=1)
    predicted = jnp.dot(landed, scatter, preferred_element_type=F32).astype(BF16)
    result_ref[0, 0] = predicted[:, 0:TILE]
    result_ref[0, 1] = predicted[:, TILE:]


def compact(data, panel_cols, aperture, operator):
    sources = panel_cols.shape[0]
    vmem = pl.BlockSpec(memory_space=pltpu.VMEM)
    dma = pltpu.SemaphoreType.DMA
    return pl.pallas_call(
        main_kernel,
        out_shape=(
            jax.ShapeDtypeStruct((2, 2, QUOTA, sources), BF16),
            jax.ShapeDtypeStruct((1, 1), jnp.int32),
        ),
        in_specs=[pl.BlockSpec(memory_space=pl.ANY)] + [vmem] * 3,
        out_specs=[vmem, pl.BlockSpec(memory_space=pltpu.SMEM)],
        scratch_shapes=[
            pltpu.VMEM((8, OWN), F32),
            pltpu.VMEM((2 * SLOTS, sources), F32),
            pltpu.VMEM((8, sources), jnp.int32),
            pltpu.VMEM((8, sources), F32),
            pltpu.VMEM((8, sources), F32),
            pltpu.VMEM((2, HEAD_K, TILE), BF16),
            pltpu.VMEM((2, TAIL_K, TILE), BF16),
            pltpu.VMEM((ACTIVE, QUOTA, 2 * TILE), BF16),
            pltpu.VMEM((GROUP, CHUNK, 2 * TILE), BF16),
            pltpu.VMEM((GROUP, CHUNK, 2 * TILE), BF16),
            pltpu.VMEM((CHUNK, 2 * TILE), BF16),
            pltpu.VMEM((COLS, CHUNK, 2 * TILE), BF16),
            pltpu.VMEM((GROUPS, ACTIVE, SLOTS, LIST), BF16),
            pltpu.VMEM((2 * SLOTS, ACTIVE * TILE), BF16),
            pltpu.VMEM((2 * TILE, WINDOW), BF16),
            pltpu.VMEM((2 * SLOTS, TILE), F32),
            pltpu.VMEM((2 * SLOTS, TILE), F32),
            pltpu.VMEM((ROWS, QUOTA, TILE), F32),
            pltpu.VMEM((QUOTA, TILE), F32),
            pltpu.VMEM((ROWS, QUOTA, TILE), F32),
            pltpu.VMEM((QUOTA, TILE), BF16),
            pltpu.VMEM((COLS, QUOTA, TILE), BF16),
            pltpu.VMEM((ROWS, QUOTA, TILE), BF16),
            pltpu.VMEM((ROWS, QUOTA, TILE), BF16),
            dma((2, 2 * LOADS)), dma((GROUP,)), dma((GROUP,)), dma((COLS,)), dma((COLS,)), dma, dma, dma, dma,
            dma((COLS,)), dma((COLS,)), dma((ROWS,)), dma((ROWS,)),
        ],
        compiler_params=pltpu.CompilerParams(
            collective_id=0, has_side_effects=True, vmem_limit_bytes=40 * 1024 * 1024
        ),
    )(data, panel_cols.reshape(1, sources), aperture.T, operator)


def subtract(operator, multiples, base_rows, mask_rows):
    sources = base_rows.shape[1]
    mult_re = multiples[:, :sources].T
    mult_im = multiples[:, sources:].T
    scale_re = operator[0][:, None]
    scale_im = operator[1][:, None]
    sub_re = scale_re * mult_re - scale_im * mult_im
    sub_im = scale_re * mult_im + scale_im * mult_re
    weight = mask_rows.astype(jnp.float32)[None]
    return base_rows.astype(jnp.float32) - weight * jnp.stack([sub_re, sub_im])


def general(data, panel_cols, aperture, operator):
    rows_dev = data.shape[1]
    receivers = data.shape[2]
    sources = panel_cols.shape[0]
    count_row = lax.axis_size("row")
    count_col = lax.axis_size("col")
    row_index = lax.axis_index("row")
    column_index = lax.axis_index("col")
    quota = receivers // count_row
    window = count_col * quota
    tile_count = rows_dev // TILE
    local_tiles = row_index * tile_count + jnp.arange(tile_count, dtype=jnp.int32)
    tile_hit = aperture[:, :, None] == local_tiles[None, None, :]
    tile_mask = jnp.any(tile_hit, axis=1)
    mask = jnp.repeat(tile_mask, TILE, axis=1).astype(jnp.bfloat16)
    own_columns = column_index * receivers + jnp.arange(receivers, dtype=jnp.int32)
    picker = (panel_cols[:, None] == own_columns[None, :]).astype(jnp.bfloat16)
    chosen = jnp.einsum("sc,zkc->zsk", picker, data, preferred_element_type=jnp.float32).astype(
        jnp.bfloat16
    )
    summed = lax.psum(chosen, "col").astype(jnp.float32)
    base = summed.astype(jnp.bfloat16) * mask[None]
    own_start = column_index * quota
    own_base = lax.dynamic_slice_in_dim(base, own_start, quota, 2)
    own_mask = lax.dynamic_slice_in_dim(mask, own_start, quota, 1)
    estimate = base
    piece = jnp.zeros((quota, 2 * sources), jnp.float32)
    for step in range(ITERS):
        current = estimate
        direct = jnp.einsum("zkc,zsk->zcs", data, current, preferred_element_type=jnp.float32)
        crossed = jnp.einsum(
            "zkc,zsk->zcs", data, current[::-1], preferred_element_type=jnp.float32
        )
        real_part = direct[0] - direct[1]
        imag_part = crossed[0] + crossed[1]
        piece = lax.psum_scatter(
            jnp.concatenate([real_part, imag_part], axis=1), "row", scatter_dimension=0, tiled=True
        )
        if step + 1 < ITERS:
            gathered = lax.all_gather(piece, "col", axis=0, tiled=True)
            fresh = subtract(operator, gathered, base[:, :, :window], mask[:, :window]).astype(
                jnp.bfloat16
            )
            estimate = jnp.concatenate([fresh, base[:, :, window:]], axis=2)
    final = subtract(operator, piece, own_base, own_mask)
    primaries = jnp.transpose(final, (0, 2, 1)).astype(jnp.bfloat16)
    predicted = jnp.transpose(piece.reshape(quota, 2, sources), (1, 0, 2)).astype(jnp.bfloat16)
    return (predicted, primaries)


def split_kernel(both_ref, first_ref, second_ref):
    first_ref[...] = both_ref[0]
    second_ref[...] = both_ref[1]


def shards(data, panel_cols, aperture, operator):
    both, fit = compact(data, panel_cols, aperture, operator)

    def keep(*_):
        return both

    def plan(*arguments):
        return jnp.stack(general(*arguments))

    both = lax.cond(fit[0, 0] > 0, keep, plan, data, panel_cols, aperture, operator)
    vmem = pl.BlockSpec(memory_space=pltpu.VMEM)
    return pl.pallas_call(
        split_kernel,
        out_shape=(jax.ShapeDtypeStruct(both.shape[1:], BF16),) * 2,
        in_specs=[vmem],
        out_specs=(vmem, vmem),
    )(both)


def solution(mesh):
    return jax.shard_map(
        shards,
        mesh=mesh,
        in_specs=(P(None, "row", "col"), P(), P(), P()),
        out_specs=(P(None, ("row", "col"), None), P(None, ("row", "col"), None)),
        check_vma=False,
    )
```

```python
import functools

import jax
import jax.numpy as jnp
from jax import lax
from jax.experimental import pallas as pl
from jax.experimental.pallas import tpu as pltpu
from jax.sharding import PartitionSpec as P

TILE = 128
ITERS = 2

MESH = pl.DeviceIdType.MESH
F32 = jnp.float32
BF16 = jnp.bfloat16
ROWS = 8
COLS = 32
BLOCK_TILES = 108
SIDE = 32
HEAD = 36
TAIL = 32
ACTIVE = HEAD + TAIL
QUOTA = 16
SLOTS = 32
GROUP = 8
GROUPS = COLS // GROUP
CHUNK = 32
LIST = GROUP * CHUNK
PAIRS = GROUPS * LIST
OWN = ACTIVE * QUOTA
WINDOW = COLS * QUOTA
LOADS = 4
SIDE_X = 4
SIDE_Z = 2
HEAD_K = HEAD * TILE
TAIL_K = TAIL * TILE
TAIL_START = (BLOCK_TILES - TAIL) * TILE


def iota(shape, dim):
    return lax.broadcasted_iota(jnp.int32, shape, dim)


def dot(left, right):
    return jnp.dot(left.astype(BF16), right.astype(BF16), preferred_element_type=F32)


def make_tables(cols_ref, ap_ref, op_ref, own_ref, pos_ref, key_ref, opa_ref, mask_ref, fit_ref):
    r = lax.axis_index("row")
    j = lax.axis_index("col")
    after = lax.rem(r + 1, ROWS)
    cols_row = cols_ref[...]
    sources = cols_row.shape[1]
    sub = iota((sources, sources), 0)
    lane = iota((sources, sources), 1)
    eye = sub == lane
    cols_col = jnp.sum(jnp.where(eye, cols_row.astype(F32), 0.0), axis=1, keepdims=True).astype(jnp.int32)
    row_row = (cols_row & 127) >> 4
    row_col = (cols_col & 127) >> 4
    dev_row = cols_row >> 7
    dev_col = cols_col >> 7
    same = row_row == row_col
    rank_row = jnp.sum(jnp.where(same & (sub < lane), 1.0, 0.0), axis=0, keepdims=True).astype(jnp.int32)

    tile_id = jnp.where(sub < HEAD, sub + BLOCK_TILES * r, -1)
    in_tail = (sub >= 64) & (sub < 64 + TAIL)
    tile_id = jnp.where(in_tail, sub - 64 + BLOCK_TILES * r + BLOCK_TILES - TAIL, tile_id)
    hit = jnp.zeros((sources, sources), jnp.bool_)
    for n in range(ap_ref.shape[0]):
        hit = hit | (ap_ref[n:n + 1, :] == tile_id)
    hit = jnp.where(hit, 1.0, 0.0)
    low = row_row * BLOCK_TILES
    tiles = ap_ref[...]
    in_own = jnp.where((tiles >= low) & (tiles < low + BLOCK_TILES), 1.0, 0.0)
    in_own = jnp.sum(in_own, axis=0, keepdims=True)

    wide = 2 * SLOTS
    slot = iota((wide, sources), 0)
    lane64 = iota((wide, sources), 1)
    is_head = slot < SLOTS
    want_row = jnp.where(is_head, r, after)
    want_rank = jnp.where(is_head, slot, slot - SLOTS)
    select = jnp.where((row_row == want_row) & (rank_row == want_rank), 1.0, 0.0)
    grid = lax.dot_general(
        select.astype(BF16), hit.astype(BF16), (((1,), (1,)), ((), ())), preferred_element_type=F32
    )
    grid = jnp.where(is_head == (lane64 < 64), grid, 0.0)
    before = dot(grid, jnp.where(sub < lane, 1.0, 0.0))
    count = jnp.sum(grid, axis=1, keepdims=True)
    group_of = jnp.where((dev_col >> 3) == lane, 1.0, 0.0)
    slot_group = dot(select, group_of)
    earlier = jnp.where(iota((wide, wide), 1) < iota((wide, wide), 0), 1.0, 0.0)
    running = dot(earlier, count * slot_group)
    offset = jnp.sum(slot_group * running, axis=1, keepdims=True)
    inside = before + offset
    valid = grid > 0.5
    slot_dev = jnp.sum(select * dev_row.astype(F32), axis=1, keepdims=True)
    slot_in = jnp.sum(select * (cols_row & 15).astype(F32), axis=1, keepdims=True)
    filled = jnp.sum(select, axis=1, keepdims=True) > 0.5
    mine = filled & (slot_dev == j.astype(F32))
    own_col = jnp.where(mine & (slot_in == lane64.astype(F32)), 1.0, 0.0)
    entry = iota((sources, OWN), 1)
    entry_tile = entry >> 4
    entry_lane = jnp.where(entry_tile < HEAD, entry_tile, entry_tile - HEAD + 64)
    spread = jnp.where(iota((sources, OWN), 0) == entry_lane, 1.0, 0.0)
    spread_col = jnp.where(iota((sources, OWN), 0) == (entry & 15), 1.0, 0.0)
    placed = jnp.where(valid, inside + 1.0, 0.0)
    own = jnp.sum(dot(placed, spread) * dot(own_col, spread_col), axis=0, keepdims=True) - 1.0
    own_ref[...] = jnp.broadcast_to(own, own_ref.shape)

    def finish():
        rank_col = jnp.sum(jnp.where(same & (lane < sub), 1.0, 0.0), axis=1, keepdims=True).astype(jnp.int32)
        group_id = jnp.sum(slot_group * lane64.astype(F32), axis=1, keepdims=True)
        inner = inside.astype(jnp.int32)
        holder = inner >> 5
        order = (holder & 3) * GROUP + group_id.astype(jnp.int32) * 2 + (holder >> 2)
        pos_ref[...] = jnp.where(valid, (order * CHUNK + (inner & (CHUNK - 1))).astype(F32), -1.0)

        key_ref[...] = jnp.broadcast_to(row_row * TILE + rank_row, key_ref.shape)

        slot_lane = lane & (SLOTS - 1)
        place = jnp.where((row_col == r) & (rank_col == slot_lane) & (lane < 2 * SLOTS), 1.0, 0.0)
        op_re = jnp.sum(jnp.where(eye, op_ref[0:1, :], 0.0), axis=1, keepdims=True)
        op_im = jnp.sum(jnp.where(eye, op_ref[1:2, :], 0.0), axis=1, keepdims=True)
        same_part = jnp.sum(place * op_re, axis=0, keepdims=True)
        cross_part = jnp.sum(place * op_im, axis=0, keepdims=True)
        cross_part = jnp.where(lane[0:1] < SLOTS, -cross_part, cross_part)
        opa_ref[...] = jnp.concatenate([same_part, cross_part] + [jnp.zeros((6, sources), F32)], axis=0)
        window_tile = j >> 3
        mask_row = jnp.sum(jnp.where(sub == window_tile, hit, 0.0), axis=0, keepdims=True)
        mask_col = jnp.sum(jnp.where(eye, mask_row, 0.0), axis=1, keepdims=True)
        mask_ref[...] = jnp.broadcast_to(jnp.sum(place * mask_col, axis=0, keepdims=True), mask_ref.shape)

        cell = iota((ROWS * GROUPS, sources), 0)
        head_cell = row_row * GROUPS + (dev_row >> 3)
        tail_cell = ((row_row + ROWS - 1) & (ROWS - 1)) * GROUPS + (dev_row >> 3)
        total = float(ap_ref.shape[0])
        load = jnp.where(cell == head_cell, in_own, 0.0) + jnp.where(cell == tail_cell, total - in_own, 0.0)
        load = jnp.sum(load, axis=1, keepdims=True)
        bad = jnp.sum(jnp.where(load > LIST, 1.0, 0.0)) + jnp.sum(jnp.where(rank_row >= SLOTS, 1.0, 0.0))
        fit_ref[0, 0] = jnp.where(bad > 0.0, 0, 1)

    return finish


def main_kernel(
    data_ref, cols_in_ref, ap_ref, op_ref, result_ref, fit_ref,
    own_ref, pos_ref, key_ref, opa_ref, mask_ref,
    head_ref, tail_ref, cols_ref, send_ref, recv_ref, chunk_ref, pairs_ref, pick_ref, est_ref,
    flip_ref, part_ref, carry_ref, first_ref, early_ref, turn_ref, fresh_ref, window_ref, out_ref, in_ref,
    load_sem, rs_send, rs_recv, ag_send, ag_recv, ur_send, ur_recv, up_send, up_recv, fr_send, fr_recv, fin_send, fin_recv,
):
    r = lax.axis_index("row")
    j = lax.axis_index("col")
    x = j // GROUP
    y = j % GROUP
    z_at = y // SIDE_X
    y_at = y % SIDE_X
    after = lax.rem(r + 1, ROWS)
    before = lax.rem(r + ROWS - 1, ROWS)

    def load(i):
        part = i // LOADS
        piece = i % LOADS
        head = pl.ds(piece * (HEAD_K // LOADS), HEAD_K // LOADS)
        tail = pl.ds(piece * (TAIL_K // LOADS), TAIL_K // LOADS)
        far = pl.ds(TAIL_START + piece * (TAIL_K // LOADS), TAIL_K // LOADS)
        return (
            pltpu.make_async_copy(data_ref.at[part, head], head_ref.at[part, head], load_sem.at[0, i]),
            pltpu.make_async_copy(data_ref.at[part, far], tail_ref.at[part, tail], load_sem.at[1, i]),
        )

    for which in range(2):
        for i in range(2 * LOADS):
            load(i)[which].start()

    barrier = pltpu.get_barrier_semaphore()

    def greet_col(i, _):
        pl.semaphore_signal(barrier, inc=1, device_id=(r, (j + i) % COLS), device_id_type=MESH)
        return 0

    def greet_row(i, _):
        pl.semaphore_signal(barrier, inc=1, device_id=((r + i) % ROWS, j), device_id_type=MESH)
        return 0

    lax.fori_loop(1, COLS, greet_col, 0)
    lax.fori_loop(1, ROWS, greet_row, 0)

    for i in range(2 * LOADS):
        load(i)[0].wait()
    for i in range(2 * LOADS):
        load(i)[1].wait()
    finish_tables = make_tables(cols_in_ref, ap_ref, op_ref, own_ref, pos_ref, key_ref, opa_ref, mask_ref, fit_ref)

    line = iota((QUOTA, TILE), 0)
    where = iota((QUOTA, TILE), 1)

    def picker(first):
        hot = jnp.where(where == line + QUOTA * first, 1.0, 0.0).astype(BF16)
        none = jnp.zeros((QUOTA, TILE), BF16)
        return jnp.concatenate(
            [jnp.concatenate([hot, none], axis=1), jnp.concatenate([none, hot], axis=1)], axis=0
        )

    def extract(source, first, base, width):
        hot = picker(first)

        def body(i, _):
            rows = pl.ds(i * width * TILE, width * TILE)
            block = jnp.concatenate([source[0, rows, :], source[1, rows, :]], axis=1)
            got = lax.dot_general(hot, block, (((1,), (1,)), ((), ())), preferred_element_type=F32).astype(BF16)
            for t in range(width):
                for part in range(2):
                    cols_ref[base + width * i + t, :, part * TILE:(part + 1) * TILE] = got[
                        part * QUOTA:(part + 1) * QUOTA, t * TILE:(t + 1) * TILE
                    ]
            return 0

        return body

    for i in range(HEAD // 12):
        extract(head_ref, r, 0, 12)(i, 0)
    for i in range(TAIL // 8):
        extract(tail_ref, after, HEAD, 8)(i, 0)

    own = own_ref[0:1, :].astype(jnp.int32)
    gather = jnp.where(own == iota((LIST, OWN), 0), 1.0, 0.0).astype(BF16)
    listed = jnp.dot(gather, cols_ref[...].reshape(OWN, 2 * TILE), preferred_element_type=F32).astype(BF16)
    send_ref[...] = listed.reshape(GROUP, CHUNK, 2 * TILE)

    pl.semaphore_wait(barrier, COLS + ROWS - 2)

    def rs_copy(i):
        to = (y + i) % GROUP
        return pltpu.make_async_remote_copy(
            src_ref=send_ref.at[to], dst_ref=recv_ref.at[y], send_sem=rs_send.at[to], recv_sem=rs_recv.at[y],
            device_id=(r, x * GROUP + to), device_id_type=MESH,
        )

    def rs_start(i, _):
        rs_copy(i).start()
        return 0

    for i in (6, 2, 5, 7, 4, 1, 3):
        rs_start(i, 0)

    finish_tables()

    pos = pos_ref[...]

    def place_rows(first_lane, first_row, base):
        def body(t, _):
            turned = pltpu.roll(pos, lax.rem(2 * TILE - first_lane - t, TILE), 1)
            column = turned[first_row:first_row + SLOTS, 0:1].astype(jnp.int32)
            hot = jnp.where(column == iota((SLOTS, PAIRS), 1), 1.0, 0.0).astype(BF16)
            for g in range(GROUPS):
                pick_ref[g, base + t] = hot[:, g * LIST:(g + 1) * LIST]
            return 0

        return body

    lax.fori_loop(0, HEAD, place_rows(0, 0, 0), 0, unroll=4)

    def rs_wait(i, _):
        source = (y + i) % GROUP
        pltpu.make_async_remote_copy(
            src_ref=send_ref.at[source], dst_ref=recv_ref.at[source], send_sem=rs_send.at[source],
            recv_sem=rs_recv.at[source], device_id=(r, x * GROUP + source), device_id_type=MESH,
        ).wait()
        return 0

    lax.fori_loop(1, GROUP, rs_wait, 0)

    def rs_add(i, total):
        return total + recv_ref[(y + i) % GROUP].astype(F32)

    chunk_ref[...] = lax.fori_loop(1, GROUP, rs_add, send_ref[y].astype(F32)).astype(BF16)

    def spread(source_ref, target_ref, send_sem, recv_sem, place):
        def copy(other, lands):
            return pltpu.make_async_remote_copy(
                src_ref=source_ref, dst_ref=target_ref.at[place(lands)], send_sem=send_sem.at[other],
                recv_sem=recv_sem.at[lands], device_id=(r, other), device_id_type=MESH,
            )

        def others(step):
            for a, b in ((2, 1), (2, 0), (1, 1), (3, 1), (1, 0), (3, 0), (0, 1), (0, 0)):
                if a or b or step:
                    yield (x + a) % SIDE_X * GROUP + (z_at + b) % SIDE_Z * SIDE_X + (y_at + step) % SIDE_X

        def start(step):
            for other in others(step):
                copy(other, j).start()

        def wait(step):
            for other in others(step):
                copy(other, other).wait_recv()

        def finish():
            for step in range(SIDE_X):
                for other in others(step):
                    copy(other, other).wait_send()

        return start, wait, finish

    def by_y(device):
        return device % SIDE_X * GROUP + device // GROUP * SIDE_Z + device // SIDE_X % SIDE_Z

    def as_is(device):
        return device

    ag_start, ag_wait, ag_finish = spread(chunk_ref, pairs_ref, ag_send, ag_recv, by_y)
    def ag_start_all():
        for step in (2, 1, 3, 0):
            ag_start(step)

    pl.when(r % 2 == 1)(ag_start_all)
    pairs_ref[by_y(j)] = chunk_ref[...]
    lax.fori_loop(0, TAIL // 2, place_rows(64, SLOTS, HEAD), 0, unroll=4)
    pl.when(r % 2 == 0)(ag_start_all)
    lax.fori_loop(TAIL // 2, TAIL, place_rows(64, SLOTS, HEAD), 0, unroll=4)

    window_data = jnp.concatenate([head_ref[0, 0:WINDOW, :], head_ref[1, 0:WINDOW, :]], axis=1)
    flip_ref[...] = window_data.T

    for step in (2, 1, 3, 0):
        ag_wait(step)

    def expand(first, tiles):
        def body(b, _):
            start = first + b * tiles
            rows = jnp.concatenate(
                [pick_ref[g, pl.ds(start, tiles)].reshape(tiles * SLOTS, LIST) for g in range(GROUPS)], axis=1
            )
            held = pairs_ref[...].reshape(PAIRS, 2 * TILE)
            full = jnp.dot(rows, held, preferred_element_type=F32).astype(BF16)
            for t in range(tiles):
                depth = pl.ds((start + t) * TILE, TILE)
                est_ref[0:SLOTS, depth] = full[t * SLOTS:(t + 1) * SLOTS, 0:TILE]
                est_ref[SLOTS:2 * SLOTS, depth] = full[t * SLOTS:(t + 1) * SLOTS, TILE:2 * TILE]
            return 0

        body(0, 0)
        body(1, 0)

    expand(HEAD, TAIL // 2)

    def product(source, base, start, depth):
        rows = pl.ds(start, depth)
        block = jnp.concatenate([source[0, rows, :], source[1, rows, :]], axis=1)
        return jnp.dot(est_ref[:, pl.ds(base + start, depth)], block, preferred_element_type=F32)

    def multiply(source, base, start, depth, count):
        def body(i, total):
            return total + product(source, base, start + i * depth, depth)

        total = body(0, 0.0)
        for i in range(1, count):
            total = body(i, total)
        return total

    def fold(total):
        real = total[0:SLOTS, 0:TILE] - total[SLOTS:, TILE:]
        imag = total[0:SLOTS, TILE:] + total[SLOTS:, 0:TILE]
        return jnp.concatenate([real, imag], axis=0)

    blank = jnp.zeros((TILE - 2 * SLOTS, TILE), F32)

    def turn(values):
        return jnp.concatenate([values, blank], axis=0).T

    part = fold(multiply(tail_ref, HEAD_K, 0, TAIL_K // 4, 4))
    part_ref[...] = part
    first_ref[...] = turn(part).reshape(ROWS, QUOTA, TILE)
    urgent = pltpu.make_async_remote_copy(
        src_ref=first_ref.at[after], dst_ref=early_ref, send_sem=ur_send, recv_sem=ur_recv,
        device_id=(after, j), device_id_type=MESH,
    )
    urgent.start()
    up = pltpu.make_async_remote_copy(
        src_ref=part_ref, dst_ref=carry_ref, send_sem=up_send, recv_sem=up_recv,
        device_id=(after, j), device_id_type=MESH,
    )
    up.start()
    expand(0, HEAD // 2)
    first_window = fold(product(head_ref, 0, 0, WINDOW))
    rest = fold(multiply(head_ref, 0, WINDOW, (HEAD_K - WINDOW) // 4, 4))

    def swap(values):
        width = values.shape[0]
        left = pltpu.roll(values, TILE - SLOTS, 1)
        right = pltpu.roll(values, SLOTS, 1)
        return left, right, iota((width, TILE), 1) < SLOTS

    def updated(base, multiples):
        left, right, real = swap(multiples)
        swapped = jnp.where(real, left, right)
        return base - mask_ref[0:1, :] * (opa_ref[0:1, :] * multiples + opa_ref[1:2, :] * swapped)

    window_base = est_ref[:, pl.ds(pl.multiple_of(x * TILE, TILE), TILE)].astype(F32)
    turn_ref[...] = turn(window_base).reshape(ROWS, QUOTA, TILE)
    base16 = turn_ref[y]
    turn_ref[...] = turn(rest + first_window).reshape(ROWS, QUOTA, TILE)
    urgent.wait()
    fresh_ref[...] = updated(base16, turn_ref[r] + early_ref[...]).astype(BF16)

    fr_start, fr_wait, fr_finish = spread(fresh_ref, window_ref, fr_send, fr_recv, as_is)
    for step in (2, 1, 3, 0):
        fr_start(step)
    window_ref[j] = fresh_ref[...]
    ag_finish()
    target = key_ref[0:1, :]
    target = jnp.concatenate([target, target + SLOTS], axis=1)
    scatter = jnp.where(target == iota((ROWS * TILE, 2 * TILE), 0), 1.0, 0.0).astype(BF16)
    source_row = key_ref[0:1, :] - r * TILE
    own_real = jnp.where(source_row == iota((TILE, TILE), 0), 1.0, 0.0)
    own_imag = jnp.where(source_row + SLOTS == iota((TILE, TILE), 0), 1.0, 0.0)
    in_row = (source_row >= 0) & (source_row < SLOTS)
    own_scatter = jnp.concatenate(
        [jnp.where(in_row, own_real, 0.0), jnp.where(in_row, own_imag, 0.0)], axis=1
    ).astype(BF16)
    up.wait()
    rest = turn(rest + carry_ref[...])
    for step in (2, 1, 3, 0):
        fr_wait(step)

    second = jnp.dot(flip_ref[...], window_ref[...].reshape(WINDOW, TILE), preferred_element_type=F32)
    left, right, real = swap(second[TILE:])
    total = rest + second[0:TILE] + jnp.where(real, -left, right)
    total = jnp.where(iota((TILE, TILE), 1) < 2 * SLOTS, total, 0.0).reshape(ROWS, QUOTA, TILE)
    out_ref[...] = total.astype(BF16)
    turn_ref[...] = total

    def fin_start(i, _):
        to = (r + i) % ROWS
        pltpu.make_async_remote_copy(
            src_ref=out_ref.at[to], dst_ref=in_ref.at[r], send_sem=fin_send.at[to], recv_sem=fin_recv.at[r],
            device_id=(to, j), device_id_type=MESH,
        ).start()
        return 0

    for i in (4, 5, 3, 2, 6, 7, 1):
        fin_start(i, 0)
    in_ref[r] = out_ref[r]
    fr_finish()
    final = updated(base16, turn_ref[r]).astype(BF16)
    mine = jnp.dot(final, own_scatter, preferred_element_type=F32).astype(BF16)
    result_ref[1, 0] = mine[:, 0:TILE]
    result_ref[1, 1] = mine[:, TILE:]

    def fin_wait(i, _):
        other = (r + i) % ROWS
        pltpu.make_async_remote_copy(
            src_ref=out_ref.at[other], dst_ref=in_ref.at[other], send_sem=fin_send.at[other],
            recv_sem=fin_recv.at[other], device_id=(other, j), device_id_type=MESH,
        ).wait()
        return 0

    lax.fori_loop(1, ROWS, fin_wait, 0)
    landed = jnp.concatenate([in_ref[k] for k in range(ROWS)], axis=1)
    predicted = jnp.dot(landed, scatter, preferred_element_type=F32).astype(BF16)
    result_ref[0, 0] = predicted[:, 0:TILE]
    result_ref[0, 1] = predicted[:, TILE:]


def compact(data, panel_cols, aperture, operator):
    sources = panel_cols.shape[0]
    vmem = pl.BlockSpec(memory_space=pltpu.VMEM)
    dma = pltpu.SemaphoreType.DMA
    return pl.pallas_call(
        main_kernel,
        out_shape=(
            jax.ShapeDtypeStruct((2, 2, QUOTA, sources), BF16),
            jax.ShapeDtypeStruct((1, 1), jnp.int32),
        ),
        in_specs=[pl.BlockSpec(memory_space=pl.ANY)] + [vmem] * 3,
        out_specs=[vmem, pl.BlockSpec(memory_space=pltpu.SMEM)],
        scratch_shapes=[
            pltpu.VMEM((8, OWN), F32),
            pltpu.VMEM((2 * SLOTS, sources), F32),
            pltpu.VMEM((8, sources), jnp.int32),
            pltpu.VMEM((8, sources), F32),
            pltpu.VMEM((8, sources), F32),
            pltpu.VMEM((2, HEAD_K, TILE), BF16),
            pltpu.VMEM((2, TAIL_K, TILE), BF16),
            pltpu.VMEM((ACTIVE, QUOTA, 2 * TILE), BF16),
            pltpu.VMEM((GROUP, CHUNK, 2 * TILE), BF16),
            pltpu.VMEM((GROUP, CHUNK, 2 * TILE), BF16),
            pltpu.VMEM((CHUNK, 2 * TILE), BF16),
            pltpu.VMEM((COLS, CHUNK, 2 * TILE), BF16),
            pltpu.VMEM((GROUPS, ACTIVE, SLOTS, LIST), BF16),
            pltpu.VMEM((2 * SLOTS, ACTIVE * TILE), BF16),
            pltpu.VMEM((2 * TILE, WINDOW), BF16),
            pltpu.VMEM((2 * SLOTS, TILE), F32),
            pltpu.VMEM((2 * SLOTS, TILE), F32),
            pltpu.VMEM((ROWS, QUOTA, TILE), F32),
            pltpu.VMEM((QUOTA, TILE), F32),
            pltpu.VMEM((ROWS, QUOTA, TILE), F32),
            pltpu.VMEM((QUOTA, TILE), BF16),
            pltpu.VMEM((COLS, QUOTA, TILE), BF16),
            pltpu.VMEM((ROWS, QUOTA, TILE), BF16),
            pltpu.VMEM((ROWS, QUOTA, TILE), BF16),
            dma((2, 2 * LOADS)), dma((GROUP,)), dma((GROUP,)), dma((COLS,)), dma((COLS,)), dma, dma, dma, dma,
            dma((COLS,)), dma((COLS,)), dma((ROWS,)), dma((ROWS,)),
        ],
        compiler_params=pltpu.CompilerParams(
            collective_id=0, has_side_effects=True, vmem_limit_bytes=40 * 1024 * 1024
        ),
    )(data, panel_cols.reshape(1, sources), aperture.T, operator)


def subtract(operator, multiples, base_rows, mask_rows):
    sources = base_rows.shape[1]
    mult_re = multiples[:, :sources].T
    mult_im = multiples[:, sources:].T
    scale_re = operator[0][:, None]
    scale_im = operator[1][:, None]
    sub_re = scale_re * mult_re - scale_im * mult_im
    sub_im = scale_re * mult_im + scale_im * mult_re
    weight = mask_rows.astype(jnp.float32)[None]
    return base_rows.astype(jnp.float32) - weight * jnp.stack([sub_re, sub_im])


def general(data, panel_cols, aperture, operator):
    rows_dev = data.shape[1]
    receivers = data.shape[2]
    sources = panel_cols.shape[0]
    count_row = lax.axis_size("row")
    count_col = lax.axis_size("col")
    row_index = lax.axis_index("row")
    column_index = lax.axis_index("col")
    quota = receivers // count_row
    window = count_col * quota
    tile_count = rows_dev // TILE
    local_tiles = row_index * tile_count + jnp.arange(tile_count, dtype=jnp.int32)
    tile_hit = aperture[:, :, None] == local_tiles[None, None, :]
    tile_mask = jnp.any(tile_hit, axis=1)
    mask = jnp.repeat(tile_mask, TILE, axis=1).astype(jnp.bfloat16)
    own_columns = column_index * receivers + jnp.arange(receivers, dtype=jnp.int32)
    picker = (panel_cols[:, None] == own_columns[None, :]).astype(jnp.bfloat16)
    chosen = jnp.einsum("sc,zkc->zsk", picker, data, preferred_element_type=jnp.float32).astype(
        jnp.bfloat16
    )
    summed = lax.psum(chosen, "col").astype(jnp.float32)
    base = summed.astype(jnp.bfloat16) * mask[None]
    own_start = column_index * quota
    own_base = lax.dynamic_slice_in_dim(base, own_start, quota, 2)
    own_mask = lax.dynamic_slice_in_dim(mask, own_start, quota, 1)
    estimate = base
    piece = jnp.zeros((quota, 2 * sources), jnp.float32)
    for step in range(ITERS):
        current = estimate
        direct = jnp.einsum("zkc,zsk->zcs", data, current, preferred_element_type=jnp.float32)
        crossed = jnp.einsum(
            "zkc,zsk->zcs", data, current[::-1], preferred_element_type=jnp.float32
        )
        real_part = direct[0] - direct[1]
        imag_part = crossed[0] + crossed[1]
        piece = lax.psum_scatter(
            jnp.concatenate([real_part, imag_part], axis=1), "row", scatter_dimension=0, tiled=True
        )
        if step + 1 < ITERS:
            gathered = lax.all_gather(piece, "col", axis=0, tiled=True)
            fresh = subtract(operator, gathered, base[:, :, :window], mask[:, :window]).astype(
                jnp.bfloat16
            )
            estimate = jnp.concatenate([fresh, base[:, :, window:]], axis=2)
    final = subtract(operator, piece, own_base, own_mask)
    primaries = jnp.transpose(final, (0, 2, 1)).astype(jnp.bfloat16)
    predicted = jnp.transpose(piece.reshape(quota, 2, sources), (1, 0, 2)).astype(jnp.bfloat16)
    return (predicted, primaries)


def split_kernel(both_ref, first_ref, second_ref):
    first_ref[...] = both_ref[0]
    second_ref[...] = both_ref[1]


def shards(data, panel_cols, aperture, operator):
    both, fit = compact(data, panel_cols, aperture, operator)

    def keep(*_):
        return both

    def plan(*arguments):
        return jnp.stack(general(*arguments))

    both = lax.cond(fit[0, 0] > 0, keep, plan, data, panel_cols, aperture, operator)
    vmem = pl.BlockSpec(memory_space=pltpu.VMEM)
    return pl.pallas_call(
        split_kernel,
        out_shape=(jax.ShapeDtypeStruct(both.shape[1:], BF16),) * 2,
        in_specs=[vmem],
        out_specs=(vmem, vmem),
    )(both)


def solution(mesh):
    return jax.shard_map(
        shards,
        mesh=mesh,
        in_specs=(P(None, "row", "col"), P(), P(), P()),
        out_specs=(P(None, ("row", "col"), None), P(None, ("row", "col"), None)),
        check_vma=False,
    )
```

```python
import functools

import jax
import jax.numpy as jnp
from jax import lax
from jax.experimental import pallas as pl
from jax.experimental.pallas import tpu as pltpu
from jax.sharding import PartitionSpec as P

TILE = 128
ITERS = 2

MESH = pl.DeviceIdType.MESH
F32 = jnp.float32
BF16 = jnp.bfloat16
ROWS = 8
COLS = 32
BLOCK_TILES = 108
SIDE = 32
HEAD = 36
TAIL = 32
ACTIVE = HEAD + TAIL
QUOTA = 16
SLOTS = 32
GROUP = 8
GROUPS = COLS // GROUP
CHUNK = 32
LIST = GROUP * CHUNK
PAIRS = GROUPS * LIST
OWN = ACTIVE * QUOTA
WINDOW = COLS * QUOTA
LOADS = 4
SIDE_X = 4
SIDE_Z = 2
HEAD_K = HEAD * TILE
TAIL_K = TAIL * TILE
TAIL_START = (BLOCK_TILES - TAIL) * TILE


def iota(shape, dim):
    return lax.broadcasted_iota(jnp.int32, shape, dim)


def dot(left, right):
    return jnp.dot(left.astype(BF16), right.astype(BF16), preferred_element_type=F32)


def make_tables(cols_ref, ap_ref, op_ref, own_ref, pos_ref, key_ref, opa_ref, mask_ref, fit_ref):
    r = lax.axis_index("row")
    j = lax.axis_index("col")
    after = lax.rem(r + 1, ROWS)
    cols_row = cols_ref[...]
    sources = cols_row.shape[1]
    sub = iota((sources, sources), 0)
    lane = iota((sources, sources), 1)
    eye = sub == lane
    cols_col = jnp.sum(jnp.where(eye, cols_row.astype(F32), 0.0), axis=1, keepdims=True).astype(jnp.int32)
    row_row = (cols_row & 127) >> 4
    row_col = (cols_col & 127) >> 4
    dev_row = cols_row >> 7
    dev_col = cols_col >> 7
    same = row_row == row_col
    rank_row = jnp.sum(jnp.where(same & (sub < lane), 1.0, 0.0), axis=0, keepdims=True).astype(jnp.int32)

    tile_id = jnp.where(sub < HEAD, sub + BLOCK_TILES * r, -1)
    in_tail = (sub >= 64) & (sub < 64 + TAIL)
    tile_id = jnp.where(in_tail, sub - 64 + BLOCK_TILES * r + BLOCK_TILES - TAIL, tile_id)
    hit = jnp.zeros((sources, sources), jnp.bool_)
    for n in range(ap_ref.shape[0]):
        hit = hit | (ap_ref[n:n + 1, :] == tile_id)
    hit = jnp.where(hit, 1.0, 0.0)
    low = row_row * BLOCK_TILES
    tiles = ap_ref[...]
    in_own = jnp.where((tiles >= low) & (tiles < low + BLOCK_TILES), 1.0, 0.0)
    in_own = jnp.sum(in_own, axis=0, keepdims=True)

    wide = 2 * SLOTS
    slot = iota((wide, sources), 0)
    lane64 = iota((wide, sources), 1)
    is_head = slot < SLOTS
    want_row = jnp.where(is_head, r, after)
    want_rank = jnp.where(is_head, slot, slot - SLOTS)
    select = jnp.where((row_row == want_row) & (rank_row == want_rank), 1.0, 0.0)
    grid = lax.dot_general(
        select.astype(BF16), hit.astype(BF16), (((1,), (1,)), ((), ())), preferred_element_type=F32
    )
    grid = jnp.where(is_head == (lane64 < 64), grid, 0.0)
    before = dot(grid, jnp.where(sub < lane, 1.0, 0.0))
    count = jnp.sum(grid, axis=1, keepdims=True)
    group_of = jnp.where((dev_col >> 3) == lane, 1.0, 0.0)
    slot_group = dot(select, group_of)
    earlier = jnp.where(iota((wide, wide), 1) < iota((wide, wide), 0), 1.0, 0.0)
    running = dot(earlier, count * slot_group)
    offset = jnp.sum(slot_group * running, axis=1, keepdims=True)
    inside = before + offset
    valid = grid > 0.5
    slot_dev = jnp.sum(select * dev_row.astype(F32), axis=1, keepdims=True)
    slot_in = jnp.sum(select * (cols_row & 15).astype(F32), axis=1, keepdims=True)
    filled = jnp.sum(select, axis=1, keepdims=True) > 0.5
    mine = filled & (slot_dev == j.astype(F32))
    own_col = jnp.where(mine & (slot_in == lane64.astype(F32)), 1.0, 0.0)
    entry = iota((sources, OWN), 1)
    entry_tile = entry >> 4
    entry_lane = jnp.where(entry_tile < HEAD, entry_tile, entry_tile - HEAD + 64)
    spread = jnp.where(iota((sources, OWN), 0) == entry_lane, 1.0, 0.0)
    spread_col = jnp.where(iota((sources, OWN), 0) == (entry & 15), 1.0, 0.0)
    placed = jnp.where(valid, inside + 1.0, 0.0)
    own = jnp.sum(dot(placed, spread) * dot(own_col, spread_col), axis=0, keepdims=True) - 1.0
    own_ref[...] = jnp.broadcast_to(own, own_ref.shape)

    def finish():
        rank_col = jnp.sum(jnp.where(same & (lane < sub), 1.0, 0.0), axis=1, keepdims=True).astype(jnp.int32)
        group_id = jnp.sum(slot_group * lane64.astype(F32), axis=1, keepdims=True)
        inner = inside.astype(jnp.int32)
        holder = inner >> 5
        order = (holder & 3) * GROUP + group_id.astype(jnp.int32) * 2 + (holder >> 2)
        pos_ref[...] = jnp.where(valid, (order * CHUNK + (inner & (CHUNK - 1))).astype(F32), -1.0)

        key_ref[...] = jnp.broadcast_to(row_row * TILE + rank_row, key_ref.shape)

        slot_lane = lane & (SLOTS - 1)
        place = jnp.where((row_col == r) & (rank_col == slot_lane) & (lane < 2 * SLOTS), 1.0, 0.0)
        op_re = jnp.sum(jnp.where(eye, op_ref[0:1, :], 0.0), axis=1, keepdims=True)
        op_im = jnp.sum(jnp.where(eye, op_ref[1:2, :], 0.0), axis=1, keepdims=True)
        same_part = jnp.sum(place * op_re, axis=0, keepdims=True)
        cross_part = jnp.sum(place * op_im, axis=0, keepdims=True)
        cross_part = jnp.where(lane[0:1] < SLOTS, -cross_part, cross_part)
        opa_ref[...] = jnp.concatenate([same_part, cross_part] + [jnp.zeros((6, sources), F32)], axis=0)
        window_tile = j >> 3
        mask_row = jnp.sum(jnp.where(sub == window_tile, hit, 0.0), axis=0, keepdims=True)
        mask_col = jnp.sum(jnp.where(eye, mask_row, 0.0), axis=1, keepdims=True)
        mask_ref[...] = jnp.broadcast_to(jnp.sum(place * mask_col, axis=0, keepdims=True), mask_ref.shape)

        cell = iota((ROWS * GROUPS, sources), 0)
        head_cell = row_row * GROUPS + (dev_row >> 3)
        tail_cell = ((row_row + ROWS - 1) & (ROWS - 1)) * GROUPS + (dev_row >> 3)
        total = float(ap_ref.shape[0])
        load = jnp.where(cell == head_cell, in_own, 0.0) + jnp.where(cell == tail_cell, total - in_own, 0.0)
        load = jnp.sum(load, axis=1, keepdims=True)
        bad = jnp.sum(jnp.where(load > LIST, 1.0, 0.0)) + jnp.sum(jnp.where(rank_row >= SLOTS, 1.0, 0.0))
        fit_ref[0, 0] = jnp.where(bad > 0.0, 0, 1)

    return finish


def main_kernel(
    data_ref, cols_in_ref, ap_ref, op_ref, result_ref, fit_ref,
    own_ref, pos_ref, key_ref, opa_ref, mask_ref,
    head_ref, tail_ref, cols_ref, send_ref, recv_ref, chunk_ref, pairs_ref, pick_ref, est_ref,
    flip_ref, part_ref, carry_ref, first_ref, early_ref, turn_ref, fresh_ref, window_ref, out_ref, in_ref,
    load_sem, rs_send, rs_recv, ag_send, ag_recv, ur_send, ur_recv, up_send, up_recv, fr_send, fr_recv, fin_send, fin_recv,
):
    r = lax.axis_index("row")
    j = lax.axis_index("col")
    x = j // GROUP
    y = j % GROUP
    z_at = y // SIDE_X
    y_at = y % SIDE_X
    after = lax.rem(r + 1, ROWS)
    before = lax.rem(r + ROWS - 1, ROWS)

    def load(i):
        part = i // LOADS
        piece = i % LOADS
        head = pl.ds(piece * (HEAD_K // LOADS), HEAD_K // LOADS)
        tail = pl.ds(piece * (TAIL_K // LOADS), TAIL_K // LOADS)
        far = pl.ds(TAIL_START + piece * (TAIL_K // LOADS), TAIL_K // LOADS)
        return (
            pltpu.make_async_copy(data_ref.at[part, head], head_ref.at[part, head], load_sem.at[0, i]),
            pltpu.make_async_copy(data_ref.at[part, far], tail_ref.at[part, tail], load_sem.at[1, i]),
        )

    for which in range(2):
        for i in range(2 * LOADS):
            load(i)[which].start()

    barrier = pltpu.get_barrier_semaphore()

    for a, b, c in sorted(
        ((a, b, c) for a in range(SIDE_X) for b in range(SIDE_Z) for c in range(SIDE_X) if a or b or c),
        key=lambda t: -(min(t[0], SIDE_X - t[0]) + t[1] + min(t[2], SIDE_X - t[2])),
    ):
        other = (x + a) % SIDE_X * GROUP + (z_at + b) % SIDE_Z * SIDE_X + (y_at + c) % SIDE_X
        pl.semaphore_signal(barrier, inc=1, device_id=(r, other), device_id_type=MESH)
    for i in (4, 5, 3, 2, 6, 7, 1):
        pl.semaphore_signal(barrier, inc=1, device_id=((r + i) % ROWS, j), device_id_type=MESH)

    for i in range(2 * LOADS):
        load(i)[0].wait()
    for i in range(2 * LOADS):
        load(i)[1].wait()
    finish_tables = make_tables(cols_in_ref, ap_ref, op_ref, own_ref, pos_ref, key_ref, opa_ref, mask_ref, fit_ref)

    line = iota((QUOTA, TILE), 0)
    where = iota((QUOTA, TILE), 1)

    def picker(first):
        hot = jnp.where(where == line + QUOTA * first, 1.0, 0.0).astype(BF16)
        none = jnp.zeros((QUOTA, TILE), BF16)
        return jnp.concatenate(
            [jnp.concatenate([hot, none], axis=1), jnp.concatenate([none, hot], axis=1)], axis=0
        )

    def extract(source, first, base, width):
        hot = picker(first)

        def body(i, _):
            rows = pl.ds(i * width * TILE, width * TILE)
            block = jnp.concatenate([source[0, rows, :], source[1, rows, :]], axis=1)
            got = lax.dot_general(hot, block, (((1,), (1,)), ((), ())), preferred_element_type=F32).astype(BF16)
            for t in range(width):
                for part in range(2):
                    cols_ref[base + width * i + t, :, part * TILE:(part + 1) * TILE] = got[
                        part * QUOTA:(part + 1) * QUOTA, t * TILE:(t + 1) * TILE
                    ]
            return 0

        return body

    for i in range(HEAD // 12):
        extract(head_ref, r, 0, 12)(i, 0)
    for i in range(TAIL // 8):
        extract(tail_ref, after, HEAD, 8)(i, 0)

    own = own_ref[0:1, :].astype(jnp.int32)
    gather = jnp.where(own == iota((LIST, OWN), 0), 1.0, 0.0).astype(BF16)
    listed = jnp.dot(gather, cols_ref[...].reshape(OWN, 2 * TILE), preferred_element_type=F32).astype(BF16)
    send_ref[...] = listed.reshape(GROUP, CHUNK, 2 * TILE)

    pl.semaphore_wait(barrier, COLS + ROWS - 2)

    def rs_copy(i):
        to = (y + i) % GROUP
        return pltpu.make_async_remote_copy(
            src_ref=send_ref.at[to], dst_ref=recv_ref.at[y], send_sem=rs_send.at[to], recv_sem=rs_recv.at[y],
            device_id=(r, x * GROUP + to), device_id_type=MESH,
        )

    def rs_start(i, _):
        rs_copy(i).start()
        return 0

    for b, c in ((1, 2), (1, 1), (1, 3), (0, 2), (1, 0), (0, 1), (0, 3)):
        rs_start((z_at + b) % SIDE_Z * SIDE_X + (y_at + c) % SIDE_X - y + GROUP, 0)

    finish_tables()

    pos = pos_ref[...]

    def place_rows(first_lane, first_row, base):
        def body(t, _):
            turned = pltpu.roll(pos, lax.rem(2 * TILE - first_lane - t, TILE), 1)
            column = turned[first_row:first_row + SLOTS, 0:1].astype(jnp.int32)
            hot = jnp.where(column == iota((SLOTS, PAIRS), 1), 1.0, 0.0).astype(BF16)
            for g in range(GROUPS):
                pick_ref[g, base + t] = hot[:, g * LIST:(g + 1) * LIST]
            return 0

        return body


    def rs_wait(i, _):
        source = (y + i) % GROUP
        pltpu.make_async_remote_copy(
            src_ref=send_ref.at[source], dst_ref=recv_ref.at[source], send_sem=rs_send.at[source],
            recv_sem=rs_recv.at[source], device_id=(r, x * GROUP + source), device_id_type=MESH,
        ).wait()
        return 0

    for i in range(1, GROUP):
        rs_wait(i, 0)

    def rs_add(i, total):
        return total + recv_ref[(y + i) % GROUP].astype(F32)

    chunk = send_ref[y].astype(F32)
    for i in range(1, GROUP):
        chunk = rs_add(i, chunk)
    chunk_ref[...] = chunk.astype(BF16)

    def spread(source_ref, target_ref, send_sem, recv_sem, place):
        def copy(other, lands):
            return pltpu.make_async_remote_copy(
                src_ref=source_ref, dst_ref=target_ref.at[place(lands)], send_sem=send_sem.at[other],
                recv_sem=recv_sem.at[lands], device_id=(r, other), device_id_type=MESH,
            )

        def others(step):
            for a, b in ((2, 1), (2, 0), (1, 1), (3, 1), (1, 0), (3, 0), (0, 1), (0, 0)):
                if a or b or step:
                    yield (x + a) % SIDE_X * GROUP + (z_at + b) % SIDE_Z * SIDE_X + (y_at + step) % SIDE_X

        def start(step):
            for other in others(step):
                copy(other, j).start()

        def wait(step):
            for other in others(step):
                copy(other, other).wait_recv()

        def finish():
            for step in range(SIDE_X):
                for other in others(step):
                    copy(other, other).wait_send()

        return start, wait, finish

    def by_y(device):
        return device % SIDE_X * GROUP + device // GROUP * SIDE_Z + device // SIDE_X % SIDE_Z

    def as_is(device):
        return device

    ag_start, ag_wait, ag_finish = spread(chunk_ref, pairs_ref, ag_send, ag_recv, by_y)
    def ag_start_all():
        for step in (2, 1, 3, 0):
            ag_start(step)

    pl.when(r % 2 == 1)(ag_start_all)
    pairs_ref[by_y(j)] = chunk_ref[...]
    lax.fori_loop(0, TAIL // 2, place_rows(64, SLOTS, HEAD), 0, unroll=4)
    pl.when(r % 2 == 0)(ag_start_all)
    lax.fori_loop(TAIL // 2, TAIL, place_rows(64, SLOTS, HEAD), 0, unroll=4)
    lax.fori_loop(0, HEAD, place_rows(0, 0, 0), 0, unroll=4)

    window_data = jnp.concatenate([head_ref[0, 0:WINDOW, :], head_ref[1, 0:WINDOW, :]], axis=1)
    flip_ref[...] = window_data.T

    for step in (2, 1, 3, 0):
        ag_wait(step)

    def expand(first, tiles):
        def body(b, _):
            start = first + b * tiles
            rows = jnp.concatenate(
                [pick_ref[g, pl.ds(start, tiles)].reshape(tiles * SLOTS, LIST) for g in range(GROUPS)], axis=1
            )
            held = pairs_ref[...].reshape(PAIRS, 2 * TILE)
            full = jnp.dot(rows, held, preferred_element_type=F32).astype(BF16)
            for t in range(tiles):
                depth = pl.ds((start + t) * TILE, TILE)
                est_ref[0:SLOTS, depth] = full[t * SLOTS:(t + 1) * SLOTS, 0:TILE]
                est_ref[SLOTS:2 * SLOTS, depth] = full[t * SLOTS:(t + 1) * SLOTS, TILE:2 * TILE]
            return 0

        body(0, 0)
        body(1, 0)

    expand(HEAD, TAIL // 2)

    def product(source, base, start, depth):
        rows = pl.ds(start, depth)
        block = jnp.concatenate([source[0, rows, :], source[1, rows, :]], axis=1)
        return jnp.dot(est_ref[:, pl.ds(base + start, depth)], block, preferred_element_type=F32)

    def multiply(source, base, start, depth, count):
        def body(i, total):
            return total + product(source, base, start + i * depth, depth)

        total = body(0, 0.0)
        for i in range(1, count):
            total = body(i, total)
        return total

    def fold(total):
        real = total[0:SLOTS, 0:TILE] - total[SLOTS:, TILE:]
        imag = total[0:SLOTS, TILE:] + total[SLOTS:, 0:TILE]
        return jnp.concatenate([real, imag], axis=0)

    blank = jnp.zeros((TILE - 2 * SLOTS, TILE), F32)

    def turn(values):
        return jnp.concatenate([values, blank], axis=0).T

    part = fold(multiply(tail_ref, HEAD_K, 0, TAIL_K // 4, 4))
    part_ref[...] = part
    first_ref[...] = turn(part).reshape(ROWS, QUOTA, TILE)
    urgent = pltpu.make_async_remote_copy(
        src_ref=first_ref.at[after], dst_ref=early_ref, send_sem=ur_send, recv_sem=ur_recv,
        device_id=(after, j), device_id_type=MESH,
    )
    urgent.start()
    up = pltpu.make_async_remote_copy(
        src_ref=part_ref, dst_ref=carry_ref, send_sem=up_send, recv_sem=up_recv,
        device_id=(after, j), device_id_type=MESH,
    )
    up.start()
    expand(0, HEAD // 2)
    first_window = fold(product(head_ref, 0, 0, WINDOW))
    rest = fold(multiply(head_ref, 0, WINDOW, (HEAD_K - WINDOW) // 4, 4))

    def swap(values):
        width = values.shape[0]
        left = pltpu.roll(values, TILE - SLOTS, 1)
        right = pltpu.roll(values, SLOTS, 1)
        return left, right, iota((width, TILE), 1) < SLOTS

    def updated(base, multiples):
        left, right, real = swap(multiples)
        swapped = jnp.where(real, left, right)
        return base - mask_ref[0:1, :] * (opa_ref[0:1, :] * multiples + opa_ref[1:2, :] * swapped)

    window_base = est_ref[:, pl.ds(pl.multiple_of(x * TILE, TILE), TILE)].astype(F32)
    turn_ref[...] = turn(window_base).reshape(ROWS, QUOTA, TILE)
    base16 = turn_ref[y]
    turn_ref[...] = turn(rest + first_window).reshape(ROWS, QUOTA, TILE)
    urgent.wait()
    fresh_ref[...] = updated(base16, turn_ref[r] + early_ref[...]).astype(BF16)

    fr_start, fr_wait, fr_finish = spread(fresh_ref, window_ref, fr_send, fr_recv, as_is)
    for a, b, c in sorted(
        ((a, b, c) for a in range(SIDE_X) for b in range(SIDE_Z) for c in range(SIDE_X) if a or b or c),
        key=lambda t: -(min(t[0], SIDE_X - t[0]) + t[1] + min(t[2], SIDE_X - t[2])),
    ):
        to = (x + a) % SIDE_X * GROUP + (z_at + b) % SIDE_Z * SIDE_X + (y_at + c) % SIDE_X
        pltpu.make_async_remote_copy(
            src_ref=fresh_ref, dst_ref=window_ref.at[j], send_sem=fr_send.at[to], recv_sem=fr_recv.at[j],
            device_id=(r, to), device_id_type=MESH,
        ).start()
    window_ref[j] = fresh_ref[...]
    ag_finish()
    target = key_ref[0:1, :]
    target = jnp.concatenate([target, target + SLOTS], axis=1)
    scatter = jnp.where(target == iota((ROWS * TILE, 2 * TILE), 0), 1.0, 0.0).astype(BF16)
    source_row = key_ref[0:1, :] - r * TILE
    own_real = jnp.where(source_row == iota((TILE, TILE), 0), 1.0, 0.0)
    own_imag = jnp.where(source_row + SLOTS == iota((TILE, TILE), 0), 1.0, 0.0)
    in_row = (source_row >= 0) & (source_row < SLOTS)
    own_scatter = jnp.concatenate(
        [jnp.where(in_row, own_real, 0.0), jnp.where(in_row, own_imag, 0.0)], axis=1
    ).astype(BF16)
    up.wait()
    rest = turn(rest + carry_ref[...])
    for step in (2, 1, 3, 0):
        fr_wait(step)

    second = jnp.dot(flip_ref[...], window_ref[...].reshape(WINDOW, TILE), preferred_element_type=F32)
    left, right, real = swap(second[TILE:])
    total = rest + second[0:TILE] + jnp.where(real, -left, right)
    total = jnp.where(iota((TILE, TILE), 1) < 2 * SLOTS, total, 0.0).reshape(ROWS, QUOTA, TILE)
    out_ref[...] = total.astype(BF16)
    turn_ref[...] = total

    def fin_start(i, _):
        to = (r + i) % ROWS
        pltpu.make_async_remote_copy(
            src_ref=out_ref.at[to], dst_ref=in_ref.at[r], send_sem=fin_send.at[to], recv_sem=fin_recv.at[r],
            device_id=(to, j), device_id_type=MESH,
        ).start()
        return 0

    for i in (4, 5, 3, 2, 6, 7, 1):
        fin_start(i, 0)
    in_ref[r] = out_ref[r]
    fr_finish()
    final = updated(base16, turn_ref[r]).astype(BF16)
    mine = jnp.dot(final, own_scatter, preferred_element_type=F32).astype(BF16)
    result_ref[1, 0] = mine[:, 0:TILE]
    result_ref[1, 1] = mine[:, TILE:]

    def fin_wait(i, _):
        other = (r + i) % ROWS
        pltpu.make_async_remote_copy(
            src_ref=out_ref.at[other], dst_ref=in_ref.at[other], send_sem=fin_send.at[other],
            recv_sem=fin_recv.at[other], device_id=(other, j), device_id_type=MESH,
        ).wait()
        return 0

    lax.fori_loop(1, ROWS, fin_wait, 0)
    landed = jnp.concatenate([in_ref[k] for k in range(ROWS)], axis=1)
    predicted = jnp.dot(landed, scatter, preferred_element_type=F32).astype(BF16)
    result_ref[0, 0] = predicted[:, 0:TILE]
    result_ref[0, 1] = predicted[:, TILE:]


def compact(data, panel_cols, aperture, operator):
    sources = panel_cols.shape[0]
    vmem = pl.BlockSpec(memory_space=pltpu.VMEM)
    dma = pltpu.SemaphoreType.DMA
    return pl.pallas_call(
        main_kernel,
        out_shape=(
            jax.ShapeDtypeStruct((2, 2, QUOTA, sources), BF16),
            jax.ShapeDtypeStruct((1, 1), jnp.int32),
        ),
        in_specs=[pl.BlockSpec(memory_space=pl.ANY)] + [vmem] * 3,
        out_specs=[vmem, pl.BlockSpec(memory_space=pltpu.SMEM)],
        scratch_shapes=[
            pltpu.VMEM((8, OWN), F32),
            pltpu.VMEM((2 * SLOTS, sources), F32),
            pltpu.VMEM((8, sources), jnp.int32),
            pltpu.VMEM((8, sources), F32),
            pltpu.VMEM((8, sources), F32),
            pltpu.VMEM((2, HEAD_K, TILE), BF16),
            pltpu.VMEM((2, TAIL_K, TILE), BF16),
            pltpu.VMEM((ACTIVE, QUOTA, 2 * TILE), BF16),
            pltpu.VMEM((GROUP, CHUNK, 2 * TILE), BF16),
            pltpu.VMEM((GROUP, CHUNK, 2 * TILE), BF16),
            pltpu.VMEM((CHUNK, 2 * TILE), BF16),
            pltpu.VMEM((COLS, CHUNK, 2 * TILE), BF16),
            pltpu.VMEM((GROUPS, ACTIVE, SLOTS, LIST), BF16),
            pltpu.VMEM((2 * SLOTS, ACTIVE * TILE), BF16),
            pltpu.VMEM((2 * TILE, WINDOW), BF16),
            pltpu.VMEM((2 * SLOTS, TILE), F32),
            pltpu.VMEM((2 * SLOTS, TILE), F32),
            pltpu.VMEM((ROWS, QUOTA, TILE), F32),
            pltpu.VMEM((QUOTA, TILE), F32),
            pltpu.VMEM((ROWS, QUOTA, TILE), F32),
            pltpu.VMEM((QUOTA, TILE), BF16),
            pltpu.VMEM((COLS, QUOTA, TILE), BF16),
            pltpu.VMEM((ROWS, QUOTA, TILE), BF16),
            pltpu.VMEM((ROWS, QUOTA, TILE), BF16),
            dma((2, 2 * LOADS)), dma((GROUP,)), dma((GROUP,)), dma((COLS,)), dma((COLS,)), dma, dma, dma, dma,
            dma((COLS,)), dma((COLS,)), dma((ROWS,)), dma((ROWS,)),
        ],
        compiler_params=pltpu.CompilerParams(
            collective_id=0, has_side_effects=True, vmem_limit_bytes=40 * 1024 * 1024
        ),
    )(data, panel_cols.reshape(1, sources), aperture.T, operator)


def subtract(operator, multiples, base_rows, mask_rows):
    sources = base_rows.shape[1]
    mult_re = multiples[:, :sources].T
    mult_im = multiples[:, sources:].T
    scale_re = operator[0][:, None]
    scale_im = operator[1][:, None]
    sub_re = scale_re * mult_re - scale_im * mult_im
    sub_im = scale_re * mult_im + scale_im * mult_re
    weight = mask_rows.astype(jnp.float32)[None]
    return base_rows.astype(jnp.float32) - weight * jnp.stack([sub_re, sub_im])


def general(data, panel_cols, aperture, operator):
    rows_dev = data.shape[1]
    receivers = data.shape[2]
    sources = panel_cols.shape[0]
    count_row = lax.axis_size("row")
    count_col = lax.axis_size("col")
    row_index = lax.axis_index("row")
    column_index = lax.axis_index("col")
    quota = receivers // count_row
    window = count_col * quota
    tile_count = rows_dev // TILE
    local_tiles = row_index * tile_count + jnp.arange(tile_count, dtype=jnp.int32)
    tile_hit = aperture[:, :, None] == local_tiles[None, None, :]
    tile_mask = jnp.any(tile_hit, axis=1)
    mask = jnp.repeat(tile_mask, TILE, axis=1).astype(jnp.bfloat16)
    own_columns = column_index * receivers + jnp.arange(receivers, dtype=jnp.int32)
    picker = (panel_cols[:, None] == own_columns[None, :]).astype(jnp.bfloat16)
    chosen = jnp.einsum("sc,zkc->zsk", picker, data, preferred_element_type=jnp.float32).astype(
        jnp.bfloat16
    )
    summed = lax.psum(chosen, "col").astype(jnp.float32)
    base = summed.astype(jnp.bfloat16) * mask[None]
    own_start = column_index * quota
    own_base = lax.dynamic_slice_in_dim(base, own_start, quota, 2)
    own_mask = lax.dynamic_slice_in_dim(mask, own_start, quota, 1)
    estimate = base
    piece = jnp.zeros((quota, 2 * sources), jnp.float32)
    for step in range(ITERS):
        current = estimate
        direct = jnp.einsum("zkc,zsk->zcs", data, current, preferred_element_type=jnp.float32)
        crossed = jnp.einsum(
            "zkc,zsk->zcs", data, current[::-1], preferred_element_type=jnp.float32
        )
        real_part = direct[0] - direct[1]
        imag_part = crossed[0] + crossed[1]
        piece = lax.psum_scatter(
            jnp.concatenate([real_part, imag_part], axis=1), "row", scatter_dimension=0, tiled=True
        )
        if step + 1 < ITERS:
            gathered = lax.all_gather(piece, "col", axis=0, tiled=True)
            fresh = subtract(operator, gathered, base[:, :, :window], mask[:, :window]).astype(
                jnp.bfloat16
            )
            estimate = jnp.concatenate([fresh, base[:, :, window:]], axis=2)
    final = subtract(operator, piece, own_base, own_mask)
    primaries = jnp.transpose(final, (0, 2, 1)).astype(jnp.bfloat16)
    predicted = jnp.transpose(piece.reshape(quota, 2, sources), (1, 0, 2)).astype(jnp.bfloat16)
    return (predicted, primaries)


def split_kernel(both_ref, first_ref, second_ref):
    first_ref[...] = both_ref[0]
    second_ref[...] = both_ref[1]


def shards(data, panel_cols, aperture, operator):
    both, fit = compact(data, panel_cols, aperture, operator)

    vmem = pl.BlockSpec(memory_space=pltpu.VMEM)

    def keep(*_):
        return pl.pallas_call(
            split_kernel,
            out_shape=(jax.ShapeDtypeStruct(both.shape[1:], BF16),) * 2,
            in_specs=[vmem],
            out_specs=(vmem, vmem),
        )(both)

    return lax.cond(fit[0, 0] > 0, keep, general, data, panel_cols, aperture, operator)


def solution(mesh):
    return jax.shard_map(
        shards,
        mesh=mesh,
        in_specs=(P(None, "row", "col"), P(), P(), P()),
        out_specs=(P(None, ("row", "col"), None), P(None, ("row", "col"), None)),
        check_vma=False,
    )
```

```python
import functools

import jax
import jax.numpy as jnp
from jax import lax
from jax.experimental import pallas as pl
from jax.experimental.pallas import tpu as pltpu
from jax.sharding import PartitionSpec as P

TILE = 128
ITERS = 2

MESH = pl.DeviceIdType.MESH
F32 = jnp.float32
BF16 = jnp.bfloat16
ROWS = 8
COLS = 32
BLOCK_TILES = 108
SIDE = 32
HEAD = 36
TAIL = 32
ACTIVE = HEAD + TAIL
QUOTA = 16
SLOTS = 32
GROUP = 8
GROUPS = COLS // GROUP
CHUNK = 32
LIST = GROUP * CHUNK
PAIRS = GROUPS * LIST
OWN = ACTIVE * QUOTA
WINDOW = COLS * QUOTA
LOADS = 4
SIDE_X = 4
SIDE_Z = 2
HEAD_K = HEAD * TILE
TAIL_K = TAIL * TILE
TAIL_START = (BLOCK_TILES - TAIL) * TILE


def iota(shape, dim):
    return lax.broadcasted_iota(jnp.int32, shape, dim)


def dot(left, right):
    return jnp.dot(left.astype(BF16), right.astype(BF16), preferred_element_type=F32)


def make_tables(cols_ref, ap_ref, op_ref, own_ref, pos_ref, key_ref, opa_ref, mask_ref, fit_ref):
    r = lax.axis_index("row")
    j = lax.axis_index("col")
    after = lax.rem(r + 1, ROWS)
    cols_row = cols_ref[...]
    sources = cols_row.shape[1]
    sub = iota((sources, sources), 0)
    lane = iota((sources, sources), 1)
    eye = sub == lane
    cols_col = jnp.sum(jnp.where(eye, cols_row.astype(F32), 0.0), axis=1, keepdims=True).astype(jnp.int32)
    row_row = (cols_row & 127) >> 4
    row_col = (cols_col & 127) >> 4
    dev_row = cols_row >> 7
    dev_col = cols_col >> 7
    same = row_row == row_col
    rank_row = jnp.sum(jnp.where(same & (sub < lane), 1.0, 0.0), axis=0, keepdims=True).astype(jnp.int32)

    tile_id = jnp.where(sub < HEAD, sub + BLOCK_TILES * r, -1)
    in_tail = (sub >= 64) & (sub < 64 + TAIL)
    tile_id = jnp.where(in_tail, sub - 64 + BLOCK_TILES * r + BLOCK_TILES - TAIL, tile_id)
    hit = jnp.zeros((sources, sources), jnp.bool_)
    for n in range(ap_ref.shape[0]):
        hit = hit | (ap_ref[n:n + 1, :] == tile_id)
    hit = jnp.where(hit, 1.0, 0.0)
    low = row_row * BLOCK_TILES
    tiles = ap_ref[...]
    in_own = jnp.where((tiles >= low) & (tiles < low + BLOCK_TILES), 1.0, 0.0)
    in_own = jnp.sum(in_own, axis=0, keepdims=True)

    wide = 2 * SLOTS
    slot = iota((wide, sources), 0)
    lane64 = iota((wide, sources), 1)
    is_head = slot < SLOTS
    want_row = jnp.where(is_head, r, after)
    want_rank = jnp.where(is_head, slot, slot - SLOTS)
    select = jnp.where((row_row == want_row) & (rank_row == want_rank), 1.0, 0.0)
    grid = lax.dot_general(
        select.astype(BF16), hit.astype(BF16), (((1,), (1,)), ((), ())), preferred_element_type=F32
    )
    grid = jnp.where(is_head == (lane64 < 64), grid, 0.0)
    before = dot(grid, jnp.where(sub < lane, 1.0, 0.0))
    count = jnp.sum(grid, axis=1, keepdims=True)
    group_of = jnp.where((dev_col >> 3) == lane, 1.0, 0.0)
    slot_group = dot(select, group_of)
    earlier = jnp.where(iota((wide, wide), 1) < iota((wide, wide), 0), 1.0, 0.0)
    running = dot(earlier, count * slot_group)
    offset = jnp.sum(slot_group * running, axis=1, keepdims=True)
    inside = before + offset
    valid = grid > 0.5
    slot_dev = jnp.sum(select * dev_row.astype(F32), axis=1, keepdims=True)
    slot_in = jnp.sum(select * (cols_row & 15).astype(F32), axis=1, keepdims=True)
    filled = jnp.sum(select, axis=1, keepdims=True) > 0.5
    mine = filled & (slot_dev == j.astype(F32))
    own_col = jnp.where(mine & (slot_in == lane64.astype(F32)), 1.0, 0.0)
    entry = iota((sources, OWN), 1)
    entry_tile = entry >> 4
    entry_lane = jnp.where(entry_tile < HEAD, entry_tile, entry_tile - HEAD + 64)
    spread = jnp.where(iota((sources, OWN), 0) == entry_lane, 1.0, 0.0)
    spread_col = jnp.where(iota((sources, OWN), 0) == (entry & 15), 1.0, 0.0)
    placed = jnp.where(valid, inside + 1.0, 0.0)
    own = jnp.sum(dot(placed, spread) * dot(own_col, spread_col), axis=0, keepdims=True) - 1.0
    own_ref[...] = jnp.broadcast_to(own, own_ref.shape)

    def finish():
        rank_col = jnp.sum(jnp.where(same & (lane < sub), 1.0, 0.0), axis=1, keepdims=True).astype(jnp.int32)
        group_id = jnp.sum(slot_group * lane64.astype(F32), axis=1, keepdims=True)
        inner = inside.astype(jnp.int32)
        holder = inner >> 5
        order = (holder & 3) * GROUP + group_id.astype(jnp.int32) * 2 + (holder >> 2)
        pos_ref[...] = jnp.where(valid, (order * CHUNK + (inner & (CHUNK - 1))).astype(F32), -1.0)

        key_ref[...] = jnp.broadcast_to(row_row * TILE + rank_row, key_ref.shape)

        slot_lane = lane & (SLOTS - 1)
        place = jnp.where((row_col == r) & (rank_col == slot_lane) & (lane < 2 * SLOTS), 1.0, 0.0)
        op_re = jnp.sum(jnp.where(eye, op_ref[0:1, :], 0.0), axis=1, keepdims=True)
        op_im = jnp.sum(jnp.where(eye, op_ref[1:2, :], 0.0), axis=1, keepdims=True)
        same_part = jnp.sum(place * op_re, axis=0, keepdims=True)
        cross_part = jnp.sum(place * op_im, axis=0, keepdims=True)
        cross_part = jnp.where(lane[0:1] < SLOTS, -cross_part, cross_part)
        opa_ref[...] = jnp.concatenate([same_part, cross_part] + [jnp.zeros((6, sources), F32)], axis=0)
        window_tile = j >> 3
        mask_row = jnp.sum(jnp.where(sub == window_tile, hit, 0.0), axis=0, keepdims=True)
        mask_col = jnp.sum(jnp.where(eye, mask_row, 0.0), axis=1, keepdims=True)
        mask_ref[...] = jnp.broadcast_to(jnp.sum(place * mask_col, axis=0, keepdims=True), mask_ref.shape)

        cell = iota((ROWS * GROUPS, sources), 0)
        head_cell = row_row * GROUPS + (dev_row >> 3)
        tail_cell = ((row_row + ROWS - 1) & (ROWS - 1)) * GROUPS + (dev_row >> 3)
        total = float(ap_ref.shape[0])
        load = jnp.where(cell == head_cell, in_own, 0.0) + jnp.where(cell == tail_cell, total - in_own, 0.0)
        load = jnp.sum(load, axis=1, keepdims=True)
        bad = jnp.sum(jnp.where(load > LIST, 1.0, 0.0)) + jnp.sum(jnp.where(rank_row >= SLOTS, 1.0, 0.0))
        fit_ref[0, 0] = jnp.where(bad > 0.0, 0, 1)

    return finish


def main_kernel(
    data_ref, cols_in_ref, ap_ref, op_ref, result_ref, fit_ref,
    own_ref, pos_ref, key_ref, opa_ref, mask_ref,
    head_ref, tail_ref, cols_ref, send_ref, recv_ref, chunk_ref, pairs_ref, pick_ref, est_ref,
    flip_ref, part_ref, carry_ref, first_ref, early_ref, turn_ref, fresh_ref, window_ref, out_ref, in_ref,
    load_sem, rs_send, rs_recv, ag_send, ag_recv, ur_send, ur_recv, up_send, up_recv, fr_send, fr_recv, fin_send, fin_recv,
):
    r = lax.axis_index("row")
    j = lax.axis_index("col")
    x = j // GROUP
    y = j % GROUP
    z_at = y // SIDE_X
    y_at = y % SIDE_X
    after = lax.rem(r + 1, ROWS)
    before = lax.rem(r + ROWS - 1, ROWS)

    def load(i):
        part = i // LOADS
        piece = i % LOADS
        head = pl.ds(piece * (HEAD_K // LOADS), HEAD_K // LOADS)
        tail = pl.ds(piece * (TAIL_K // LOADS), TAIL_K // LOADS)
        far = pl.ds(TAIL_START + piece * (TAIL_K // LOADS), TAIL_K // LOADS)
        return (
            pltpu.make_async_copy(data_ref.at[part, head], head_ref.at[part, head], load_sem.at[0, i]),
            pltpu.make_async_copy(data_ref.at[part, far], tail_ref.at[part, tail], load_sem.at[1, i]),
        )

    for which in range(2):
        for i in range(2 * LOADS):
            load(i)[which].start()

    barrier = pltpu.get_barrier_semaphore()

    for a, b, c in sorted(
        ((a, b, c) for a in range(SIDE_X) for b in range(SIDE_Z) for c in range(SIDE_X) if a or b or c),
        key=lambda t: -(min(t[0], SIDE_X - t[0]) + t[1] + min(t[2], SIDE_X - t[2])),
    ):
        other = (x + a) % SIDE_X * GROUP + (z_at + b) % SIDE_Z * SIDE_X + (y_at + c) % SIDE_X
        pl.semaphore_signal(barrier, inc=1, device_id=(r, other), device_id_type=MESH)
    for i in (4, 5, 3, 2, 6, 7, 1):
        pl.semaphore_signal(barrier, inc=1, device_id=((r + i) % ROWS, j), device_id_type=MESH)

    for i in range(2 * LOADS):
        load(i)[0].wait()
    for i in range(2 * LOADS):
        load(i)[1].wait()
    finish_tables = make_tables(cols_in_ref, ap_ref, op_ref, own_ref, pos_ref, key_ref, opa_ref, mask_ref, fit_ref)

    line = iota((QUOTA, TILE), 0)
    where = iota((QUOTA, TILE), 1)

    def picker(first):
        hot = jnp.where(where == line + QUOTA * first, 1.0, 0.0).astype(BF16)
        none = jnp.zeros((QUOTA, TILE), BF16)
        return jnp.concatenate(
            [jnp.concatenate([hot, none], axis=1), jnp.concatenate([none, hot], axis=1)], axis=0
        )

    def extract(source, first, base, width):
        hot = picker(first)

        def body(i, _):
            rows = pl.ds(i * width * TILE, width * TILE)
            block = jnp.concatenate([source[0, rows, :], source[1, rows, :]], axis=1)
            got = lax.dot_general(hot, block, (((1,), (1,)), ((), ())), preferred_element_type=F32).astype(BF16)
            for t in range(width):
                for part in range(2):
                    cols_ref[base + width * i + t, :, part * TILE:(part + 1) * TILE] = got[
                        part * QUOTA:(part + 1) * QUOTA, t * TILE:(t + 1) * TILE
                    ]
            return 0

        return body

    for i in range(HEAD // 12):
        extract(head_ref, r, 0, 12)(i, 0)
    for i in range(TAIL // 8):
        extract(tail_ref, after, HEAD, 8)(i, 0)

    own = own_ref[0:1, :].astype(jnp.int32)
    gather = jnp.where(own == iota((LIST, OWN), 0), 1.0, 0.0).astype(BF16)
    listed = jnp.dot(gather, cols_ref[...].reshape(OWN, 2 * TILE), preferred_element_type=F32).astype(BF16)
    send_ref[...] = listed.reshape(GROUP, CHUNK, 2 * TILE)

    pl.semaphore_wait(barrier, COLS + ROWS - 2)

    def rs_copy(i):
        to = (y + i) % GROUP
        return pltpu.make_async_remote_copy(
            src_ref=send_ref.at[to], dst_ref=recv_ref.at[y], send_sem=rs_send.at[to], recv_sem=rs_recv.at[y],
            device_id=(r, x * GROUP + to), device_id_type=MESH,
        )

    def rs_start(i, _):
        rs_copy(i).start()
        return 0

    for b, c in ((1, 2), (1, 1), (1, 3), (0, 2), (1, 0), (0, 1), (0, 3)):
        rs_start((z_at + b) % SIDE_Z * SIDE_X + (y_at + c) % SIDE_X - y + GROUP, 0)

    finish_tables()

    pos = pos_ref[...]

    def place_rows(first_lane, first_row, base):
        def body(t, _):
            turned = pltpu.roll(pos, lax.rem(2 * TILE - first_lane - t, TILE), 1)
            column = turned[first_row:first_row + SLOTS, 0:1].astype(jnp.int32)
            hot = jnp.where(column == iota((SLOTS, PAIRS), 1), 1.0, 0.0).astype(BF16)
            for g in range(GROUPS):
                pick_ref[g, base + t] = hot[:, g * LIST:(g + 1) * LIST]
            return 0

        return body


    def rs_wait(i, _):
        source = (y + i) % GROUP
        pltpu.make_async_remote_copy(
            src_ref=send_ref.at[source], dst_ref=recv_ref.at[source], send_sem=rs_send.at[source],
            recv_sem=rs_recv.at[source], device_id=(r, x * GROUP + source), device_id_type=MESH,
        ).wait()
        return 0

    for i in range(1, GROUP):
        rs_wait(i, 0)

    def rs_add(i, total):
        return total + recv_ref[(y + i) % GROUP].astype(F32)

    chunk = send_ref[y].astype(F32)
    for i in range(1, GROUP):
        chunk = rs_add(i, chunk)
    chunk_ref[...] = chunk.astype(BF16)

    def spread(source_ref, target_ref, send_sem, recv_sem, place):
        def copy(other, lands):
            return pltpu.make_async_remote_copy(
                src_ref=source_ref, dst_ref=target_ref.at[place(lands)], send_sem=send_sem.at[other],
                recv_sem=recv_sem.at[lands], device_id=(r, other), device_id_type=MESH,
            )

        def others(step):
            for a, b in ((2, 1), (2, 0), (1, 1), (3, 1), (1, 0), (3, 0), (0, 1), (0, 0)):
                if a or b or step:
                    yield (x + a) % SIDE_X * GROUP + (z_at + b) % SIDE_Z * SIDE_X + (y_at + step) % SIDE_X

        def start(step):
            for other in others(step):
                copy(other, j).start()

        def wait(step):
            for other in others(step):
                copy(other, other).wait_recv()

        def finish():
            for step in range(SIDE_X):
                for other in others(step):
                    copy(other, other).wait_send()

        return start, wait, finish

    def by_y(device):
        return device % SIDE_X * GROUP + device // GROUP * SIDE_Z + device // SIDE_X % SIDE_Z

    def as_is(device):
        return device

    ag_start, ag_wait, ag_finish = spread(chunk_ref, pairs_ref, ag_send, ag_recv, by_y)
    def ag_start_all():
        for step in (2, 1, 3, 0):
            ag_start(step)

    pl.when(r % 2 == 1)(ag_start_all)
    pairs_ref[by_y(j)] = chunk_ref[...]
    lax.fori_loop(0, TAIL // 2, place_rows(64, SLOTS, HEAD), 0, unroll=4)
    pl.when(r % 2 == 0)(ag_start_all)
    lax.fori_loop(TAIL // 2, TAIL, place_rows(64, SLOTS, HEAD), 0, unroll=4)
    lax.fori_loop(0, HEAD, place_rows(0, 0, 0), 0, unroll=4)

    window_data = jnp.concatenate([head_ref[0, 0:WINDOW, :], head_ref[1, 0:WINDOW, :]], axis=1)
    flip_ref[...] = window_data.T

    for step in (2, 1, 3, 0):
        ag_wait(step)

    def expand(first, tiles):
        def body(b, _):
            start = first + b * tiles
            rows = jnp.concatenate(
                [pick_ref[g, pl.ds(start, tiles)].reshape(tiles * SLOTS, LIST) for g in range(GROUPS)], axis=1
            )
            held = pairs_ref[...].reshape(PAIRS, 2 * TILE)
            full = jnp.dot(rows, held, preferred_element_type=F32).astype(BF16)
            for t in range(tiles):
                depth = pl.ds((start + t) * TILE, TILE)
                est_ref[0:SLOTS, depth] = full[t * SLOTS:(t + 1) * SLOTS, 0:TILE]
                est_ref[SLOTS:2 * SLOTS, depth] = full[t * SLOTS:(t + 1) * SLOTS, TILE:2 * TILE]
            return 0

        body(0, 0)
        body(1, 0)

    expand(HEAD, TAIL // 2)

    def product(source, base, start, depth):
        rows = pl.ds(start, depth)
        block = jnp.concatenate([source[0, rows, :], source[1, rows, :]], axis=1)
        return jnp.dot(est_ref[:, pl.ds(base + start, depth)], block, preferred_element_type=F32)

    def multiply(source, base, start, depth, count):
        def body(i, total):
            return total + product(source, base, start + i * depth, depth)

        total = body(0, 0.0)
        for i in range(1, count):
            total = body(i, total)
        return total

    def fold(total):
        real = total[0:SLOTS, 0:TILE] - total[SLOTS:, TILE:]
        imag = total[0:SLOTS, TILE:] + total[SLOTS:, 0:TILE]
        return jnp.concatenate([real, imag], axis=0)

    blank = jnp.zeros((TILE - 2 * SLOTS, TILE), F32)

    def turn(values):
        return jnp.concatenate([values, blank], axis=0).T

    part = fold(multiply(tail_ref, HEAD_K, 0, TAIL_K // 4, 4))
    part_ref[...] = part
    first_ref[...] = turn(part).reshape(ROWS, QUOTA, TILE)
    urgent = pltpu.make_async_remote_copy(
        src_ref=first_ref.at[after], dst_ref=early_ref, send_sem=ur_send, recv_sem=ur_recv,
        device_id=(after, j), device_id_type=MESH,
    )
    urgent.start()
    up = pltpu.make_async_remote_copy(
        src_ref=part_ref, dst_ref=carry_ref, send_sem=up_send, recv_sem=up_recv,
        device_id=(after, j), device_id_type=MESH,
    )
    expand(0, HEAD // 2)
    first_window = fold(product(head_ref, 0, 0, WINDOW))
    rest = fold(multiply(head_ref, 0, WINDOW, (HEAD_K - WINDOW) // 4, 4))

    def swap(values):
        width = values.shape[0]
        left = pltpu.roll(values, TILE - SLOTS, 1)
        right = pltpu.roll(values, SLOTS, 1)
        return left, right, iota((width, TILE), 1) < SLOTS

    def updated(base, multiples):
        left, right, real = swap(multiples)
        swapped = jnp.where(real, left, right)
        return base - mask_ref[0:1, :] * (opa_ref[0:1, :] * multiples + opa_ref[1:2, :] * swapped)

    window_base = est_ref[:, pl.ds(pl.multiple_of(x * TILE, TILE), TILE)].astype(F32)
    turn_ref[...] = turn(window_base).reshape(ROWS, QUOTA, TILE)
    base16 = turn_ref[y]
    turn_ref[...] = turn(rest + first_window).reshape(ROWS, QUOTA, TILE)
    urgent.wait()
    fresh_ref[...] = updated(base16, turn_ref[r] + early_ref[...]).astype(BF16)

    fr_start, fr_wait, fr_finish = spread(fresh_ref, window_ref, fr_send, fr_recv, as_is)
    for a, b, c in sorted(
        ((a, b, c) for a in range(SIDE_X) for b in range(SIDE_Z) for c in range(SIDE_X) if a or b or c),
        key=lambda t: -(min(t[0], SIDE_X - t[0]) + t[1] + min(t[2], SIDE_X - t[2])),
    ):
        to = (x + a) % SIDE_X * GROUP + (z_at + b) % SIDE_Z * SIDE_X + (y_at + c) % SIDE_X
        pltpu.make_async_remote_copy(
            src_ref=fresh_ref, dst_ref=window_ref.at[j], send_sem=fr_send.at[to], recv_sem=fr_recv.at[j],
            device_id=(r, to), device_id_type=MESH,
        ).start()
    up.start()
    window_ref[j] = fresh_ref[...]
    ag_finish()
    target = key_ref[0:1, :]
    target = jnp.concatenate([target, target + SLOTS], axis=1)
    scatter = jnp.where(target == iota((ROWS * TILE, 2 * TILE), 0), 1.0, 0.0).astype(BF16)
    source_row = key_ref[0:1, :] - r * TILE
    own_real = jnp.where(source_row == iota((TILE, TILE), 0), 1.0, 0.0)
    own_imag = jnp.where(source_row + SLOTS == iota((TILE, TILE), 0), 1.0, 0.0)
    in_row = (source_row >= 0) & (source_row < SLOTS)
    own_scatter = jnp.concatenate(
        [jnp.where(in_row, own_real, 0.0), jnp.where(in_row, own_imag, 0.0)], axis=1
    ).astype(BF16)
    up.wait()
    rest = turn(rest + carry_ref[...])
    for step in (2, 1, 3, 0):
        fr_wait(step)

    second = jnp.dot(flip_ref[...], window_ref[...].reshape(WINDOW, TILE), preferred_element_type=F32)
    left, right, real = swap(second[TILE:])
    total = rest + second[0:TILE] + jnp.where(real, -left, right)
    total = jnp.where(iota((TILE, TILE), 1) < 2 * SLOTS, total, 0.0).reshape(ROWS, QUOTA, TILE)
    out_ref[...] = total.astype(BF16)
    turn_ref[...] = total

    def fin_start(i, _):
        to = (r + i) % ROWS
        pltpu.make_async_remote_copy(
            src_ref=out_ref.at[to], dst_ref=in_ref.at[r], send_sem=fin_send.at[to], recv_sem=fin_recv.at[r],
            device_id=(to, j), device_id_type=MESH,
        ).start()
        return 0

    for i in (4, 5, 3, 2, 6, 7, 1):
        fin_start(i, 0)
    in_ref[r] = out_ref[r]
    fr_finish()
    final = updated(base16, turn_ref[r]).astype(BF16)
    mine = jnp.dot(final, own_scatter, preferred_element_type=F32).astype(BF16)
    result_ref[1, 0] = mine[:, 0:TILE]
    result_ref[1, 1] = mine[:, TILE:]

    def fin_wait(i, _):
        other = (r + i) % ROWS
        pltpu.make_async_remote_copy(
            src_ref=out_ref.at[other], dst_ref=in_ref.at[other], send_sem=fin_send.at[other],
            recv_sem=fin_recv.at[other], device_id=(other, j), device_id_type=MESH,
        ).wait()
        return 0

    lax.fori_loop(1, ROWS, fin_wait, 0)
    landed = jnp.concatenate([in_ref[k] for k in range(ROWS)], axis=1)
    predicted = jnp.dot(landed, scatter, preferred_element_type=F32).astype(BF16)
    result_ref[0, 0] = predicted[:, 0:TILE]
    result_ref[0, 1] = predicted[:, TILE:]


def compact(data, panel_cols, aperture, operator):
    sources = panel_cols.shape[0]
    vmem = pl.BlockSpec(memory_space=pltpu.VMEM)
    dma = pltpu.SemaphoreType.DMA
    return pl.pallas_call(
        main_kernel,
        out_shape=(
            jax.ShapeDtypeStruct((2, 2, QUOTA, sources), BF16),
            jax.ShapeDtypeStruct((1, 1), jnp.int32),
        ),
        in_specs=[pl.BlockSpec(memory_space=pl.ANY)] + [vmem] * 3,
        out_specs=[vmem, pl.BlockSpec(memory_space=pltpu.SMEM)],
        scratch_shapes=[
            pltpu.VMEM((8, OWN), F32),
            pltpu.VMEM((2 * SLOTS, sources), F32),
            pltpu.VMEM((8, sources), jnp.int32),
            pltpu.VMEM((8, sources), F32),
            pltpu.VMEM((8, sources), F32),
            pltpu.VMEM((2, HEAD_K, TILE), BF16),
            pltpu.VMEM((2, TAIL_K, TILE), BF16),
            pltpu.VMEM((ACTIVE, QUOTA, 2 * TILE), BF16),
            pltpu.VMEM((GROUP, CHUNK, 2 * TILE), BF16),
            pltpu.VMEM((GROUP, CHUNK, 2 * TILE), BF16),
            pltpu.VMEM((CHUNK, 2 * TILE), BF16),
            pltpu.VMEM((COLS, CHUNK, 2 * TILE), BF16),
            pltpu.VMEM((GROUPS, ACTIVE, SLOTS, LIST), BF16),
            pltpu.VMEM((2 * SLOTS, ACTIVE * TILE), BF16),
            pltpu.VMEM((2 * TILE, WINDOW), BF16),
            pltpu.VMEM((2 * SLOTS, TILE), F32),
            pltpu.VMEM((2 * SLOTS, TILE), F32),
            pltpu.VMEM((ROWS, QUOTA, TILE), F32),
            pltpu.VMEM((QUOTA, TILE), F32),
            pltpu.VMEM((ROWS, QUOTA, TILE), F32),
            pltpu.VMEM((QUOTA, TILE), BF16),
            pltpu.VMEM((COLS, QUOTA, TILE), BF16),
            pltpu.VMEM((ROWS, QUOTA, TILE), BF16),
            pltpu.VMEM((ROWS, QUOTA, TILE), BF16),
            dma((2, 2 * LOADS)), dma((GROUP,)), dma((GROUP,)), dma((COLS,)), dma((COLS,)), dma, dma, dma, dma,
            dma((COLS,)), dma((COLS,)), dma((ROWS,)), dma((ROWS,)),
        ],
        compiler_params=pltpu.CompilerParams(
            collective_id=0, has_side_effects=True, vmem_limit_bytes=40 * 1024 * 1024
        ),
    )(data, panel_cols.reshape(1, sources), aperture.T, operator)


def subtract(operator, multiples, base_rows, mask_rows):
    sources = base_rows.shape[1]
    mult_re = multiples[:, :sources].T
    mult_im = multiples[:, sources:].T
    scale_re = operator[0][:, None]
    scale_im = operator[1][:, None]
    sub_re = scale_re * mult_re - scale_im * mult_im
    sub_im = scale_re * mult_im + scale_im * mult_re
    weight = mask_rows.astype(jnp.float32)[None]
    return base_rows.astype(jnp.float32) - weight * jnp.stack([sub_re, sub_im])


def general(data, panel_cols, aperture, operator):
    rows_dev = data.shape[1]
    receivers = data.shape[2]
    sources = panel_cols.shape[0]
    count_row = lax.axis_size("row")
    count_col = lax.axis_size("col")
    row_index = lax.axis_index("row")
    column_index = lax.axis_index("col")
    quota = receivers // count_row
    window = count_col * quota
    tile_count = rows_dev // TILE
    local_tiles = row_index * tile_count + jnp.arange(tile_count, dtype=jnp.int32)
    tile_hit = aperture[:, :, None] == local_tiles[None, None, :]
    tile_mask = jnp.any(tile_hit, axis=1)
    mask = jnp.repeat(tile_mask, TILE, axis=1).astype(jnp.bfloat16)
    own_columns = column_index * receivers + jnp.arange(receivers, dtype=jnp.int32)
    picker = (panel_cols[:, None] == own_columns[None, :]).astype(jnp.bfloat16)
    chosen = jnp.einsum("sc,zkc->zsk", picker, data, preferred_element_type=jnp.float32).astype(
        jnp.bfloat16
    )
    summed = lax.psum(chosen, "col").astype(jnp.float32)
    base = summed.astype(jnp.bfloat16) * mask[None]
    own_start = column_index * quota
    own_base = lax.dynamic_slice_in_dim(base, own_start, quota, 2)
    own_mask = lax.dynamic_slice_in_dim(mask, own_start, quota, 1)
    estimate = base
    piece = jnp.zeros((quota, 2 * sources), jnp.float32)
    for step in range(ITERS):
        current = estimate
        direct = jnp.einsum("zkc,zsk->zcs", data, current, preferred_element_type=jnp.float32)
        crossed = jnp.einsum(
            "zkc,zsk->zcs", data, current[::-1], preferred_element_type=jnp.float32
        )
        real_part = direct[0] - direct[1]
        imag_part = crossed[0] + crossed[1]
        piece = lax.psum_scatter(
            jnp.concatenate([real_part, imag_part], axis=1), "row", scatter_dimension=0, tiled=True
        )
        if step + 1 < ITERS:
            gathered = lax.all_gather(piece, "col", axis=0, tiled=True)
            fresh = subtract(operator, gathered, base[:, :, :window], mask[:, :window]).astype(
                jnp.bfloat16
            )
            estimate = jnp.concatenate([fresh, base[:, :, window:]], axis=2)
    final = subtract(operator, piece, own_base, own_mask)
    primaries = jnp.transpose(final, (0, 2, 1)).astype(jnp.bfloat16)
    predicted = jnp.transpose(piece.reshape(quota, 2, sources), (1, 0, 2)).astype(jnp.bfloat16)
    return (predicted, primaries)


def split_kernel(both_ref, first_ref, second_ref):
    first_ref[...] = both_ref[0]
    second_ref[...] = both_ref[1]


def shards(data, panel_cols, aperture, operator):
    both, fit = compact(data, panel_cols, aperture, operator)

    vmem = pl.BlockSpec(memory_space=pltpu.VMEM)

    def keep(*_):
        return pl.pallas_call(
            split_kernel,
            out_shape=(jax.ShapeDtypeStruct(both.shape[1:], BF16),) * 2,
            in_specs=[vmem],
            out_specs=(vmem, vmem),
        )(both)

    return lax.cond(fit[0, 0] > 0, keep, general, data, panel_cols, aperture, operator)


def solution(mesh):
    return jax.shard_map(
        shards,
        mesh=mesh,
        in_specs=(P(None, "row", "col"), P(), P(), P()),
        out_specs=(P(None, ("row", "col"), None), P(None, ("row", "col"), None)),
        check_vma=False,
    )
```
